512 devices in a mesh: prompt: 8 (over y), dp: 4 (over x), expert: 16 (over z, core).
Axes of the slice: x: 4, y: 8, z: 8, core: 2. Of those that a mesh axis runs over, the one named last changes fastest.
Arguments:
- ssm_input: bfloat16 [65536, 4096], P(('prompt', 'dp', 'expert')), may hold values from -6 to 6
- b_inputs: bfloat16 [65536, 128], P(('prompt', 'dp', 'expert')), may hold values from -1.5 to 1.5
- c_readout: bfloat16 [65536, 128], P(('prompt', 'dp', 'expert')), may hold values from -1.5 to 1.5
- step_raw: float32 [65536, 64], P(('prompt', 'dp', 'expert')), may hold values from -4 to 4
- decay_rate: float32 [64], replicated, may hold values from 0.00234375 to 0.05
- skip_gain: float32 [64], replicated, may hold values from 0.25 to 1.75
- conv_weight: float32 [4, 4096], replicated, may hold values from -3 to 3
- prompt_state: bfloat16 [32, 64, 64, 128], P('expert', ('prompt', 'dp')), may hold values from -6 to 6
- prompt_taps: bfloat16 [32, 64, 192], P('expert', ('prompt', 'dp')), may hold values from -6 to 6
- group_index: int32 [512], P(('prompt', 'dp', 'expert')), may hold values from 0 to 1
- lengths: int32 [512], P(('prompt', 'dp', 'expert')), may hold values from 1 to 128
- mixed_grad: bfloat16 [65536, 4096], P(('prompt', 'dp', 'expert')), may hold values from -6 to 6
- expert_index: int32 [65536, 1], P(('prompt', 'dp', 'expert')), may hold values from 0 to 15; in each aligned block of 128 rows (0 to 127, 128 to 255, ...) at most 12 rows name the same one
- route_gain: float32 [65536, 1], P(('prompt', 'dp', 'expert')), may hold values from 0.1 to 1
- gate_weight: bfloat16 [16, 768, 4096], P('expert', ('prompt', 'dp')), may hold values from -0.09375 to 0.09375
- up_weight: bfloat16 [16, 768, 4096], P('expert', ('prompt', 'dp')), may hold values from -0.09375 to 0.09375
- down_weight: bfloat16 [16, 768, 4096], P('expert', ('prompt', 'dp')), may hold values from -0.21875 to 0.21875
Outputs:
- moe_out: bfloat16 [65536, 4096], P(('prompt', 'dp', 'expert'))
- state_grad: float32 [32, 64, 64, 128], P('expert', ('prompt', 'dp'))
- taps_grad: float32 [32, 64, 192], P('expert', ('prompt', 'dp'))
The draws below stay inside these ranges and needn't reach their ends.
Inputs may be any that keep to these rules, and one draw needn't show every extreme that they name: `expert_index`: within each response's 128 tokens no expert is named more than 12 times, a bound that some block reaches.
All inputs are finite; a program needn't handle non-finite values.
Results may differ from the reference program's by a relative error of at most 0.019.
Values may be sent and summed in bfloat16 or wider, within the bound.
No kernel may reach another device: no remote copies, remote signals or barrier semaphores. Data moves between devices by JAX's collectives and lax.ppermute only.
A program may use at most 128 MiB of HBM per device.

```python
import math
import jax
import jax.numpy as jnp
import numpy as np
from jax import lax

HEADS = 64
HEAD_DIM = 64
STATE = 128
TAPS = 4
EXP_FF = 768
TOP = 1
PROM_DEV = 2
LEN = 128
CH = 4096
EXPERTS = 16
CAP = 12
RESPONSES = 512
TOKENS = 65536
PROMPTS = 32
N_EXPERT = 16


def with_ends(values, stream_key, least, high):
    longest = values.shape.index(max(values.shape))
    spots = []
    for shift in (0, 1):
        where = [jax.random.randint(jax.random.fold_in(stream_key, axis), (), 0, length) for axis, length in enumerate(values.shape)]
        where[longest] = (where[longest] + shift) % values.shape[longest]
        spots.append(tuple(where))
    return values.at[spots[0]].set(least).at[spots[1]].set(high)


def level_of(key, extent, pieces, low, largest):
    def one(position, shards_of):
        steps = jax.random.uniform(jax.random.fold_in(jax.random.fold_in(key, 6), position), (shards_of,), jnp.float32, low / len(pieces), largest / len(pieces))
        return jnp.repeat(jnp.exp(steps), extent[position] // shards_of).reshape((-1,) + (1,) * (len(extent) - position - 1))

    level = one(*pieces[0])
    for cut in pieces[1:]:
        level = level * one(*cut)
    return level


def deal_out(key, own, number, rows, count, top, most, slope):
    order = jax.random.permutation(key, count)
    packed, usual = shares(count, rows * top, most, slope, True), shares(count, rows * top, most, slope, False)
    places = jnp.arange(count)

    def named(tallies, rotation):
        used = int((tallies > 0).sum())
        fixed = max(1, used // 4)
        moved = fixed + (places - fixed + rotation * (used - fixed)) % max(1, count - fixed)
        return jnp.zeros((count,), jnp.int32).at[order[jnp.where(places < fixed, places, moved)]].set(jnp.asarray(tallies, jnp.int32))

    tallies = jnp.where(number % 4 == 0, named(packed, number // 4), named(usual, number - number // 4 - 1))
    mixed = jax.random.permutation(jax.random.fold_in(own, 3), count)
    giver, sink = mixed[0:count // 2 * 2:2], mixed[1:count // 2 * 2:2]
    slack = jnp.minimum(tallies[giver] - 1, most - tallies[sink]) // 2
    slack = jnp.where((giver == order[0]) | (sink == order[0]) | (tallies[sink] == 0), 0, jnp.maximum(slack, 0))
    moved = jax.random.randint(jax.random.fold_in(own, 4), (count // 2,), 0, 1 << 20) % (slack + 1)
    tallies = tallies.at[giver].add(-moved).at[sink].add(moved)
    labels = jnp.searchsorted(jnp.cumsum(tallies), jnp.arange(rows * top), side="right").astype(jnp.int32)
    listing = labels.reshape(top, rows).T
    listing = listing[jax.random.permutation(jax.random.fold_in(own, 1), rows)]
    rotation = jax.random.randint(jax.random.fold_in(own, 2), (rows, 1), 0, top)
    return jnp.take_along_axis(listing, (jnp.arange(top)[None, :] + rotation) % top, axis=1)


def shares(number_of, total, limit, slope, full):
    weights = [(1 << 20) // math.isqrt(standing ** slope) + 1 for standing in range(1, number_of + 1)]
    largest = limit if full else min(limit, max(-(-total // number_of), total * weights[0] // sum(weights)))
    least = 1 if total - largest >= number_of - 1 else 0
    given, spare = [largest] + [least] * (number_of - 1), total - largest - least * (number_of - 1)
    while spare > 0:
        candidates = [i for i in range(1, number_of) if given[i] < largest] or [i for i in range(1, number_of) if given[i] < limit]
        whole, left = sum([weights[i] for i in candidates]), spare
        for i in candidates:
            more = min(limit - given[i], max(1, left * weights[i] // whole), spare)
            given[i] = given[i] + more
            spare = spare - more
    return np.array(given)


def centred(key, extent, spread, reach, shards=(), dtype=jnp.bfloat16):
    values = jax.random.normal(key, extent, jnp.float32) * spread
    if len(shards) > 0:
        values = level_of(key, extent, shards, -0.22, 0.18) * values
    return jnp.clip(values, min=-reach, max=reach).astype(dtype)


def setup_inputs(seed: int = 0) -> dict:
    key_list = jax.random.split(jax.random.key(seed), 18)
    ssm_input = centred(key_list[0], (TOKENS, CH), 1.0, 6.0, ((0, 512),))
    b_inputs = centred(key_list[1], (TOKENS, STATE), 0.25, 1.5, ((0, 512),))
    c_readout = centred(key_list[2], (TOKENS, STATE), 0.25, 1.5, ((0, 512),))
    step_raw = centred(key_list[3], (TOKENS, HEADS), 1.0, 4.0, ((0, 512),), jnp.float32)
    decay_rate = jnp.clip(jnp.exp(jax.random.uniform(key_list[4], (HEADS,), jnp.float32, math.log(0.00234375), math.log(0.05))), 0.00234375, 0.05)
    skip_gain = jnp.clip(1.0 + 0.15 * jax.random.normal(key_list[5], (HEADS,), jnp.float32), 0.25, 1.75)
    conv_weight = centred(key_list[6], (TAPS, CH), 0.5, 3.0, (), jnp.float32)
    prompt_state = centred(key_list[7], (PROMPTS, HEADS, HEAD_DIM, STATE), 1.0, 6.0, ((0, 16), (1, 32)))
    prompt_taps = centred(key_list[8], (PROMPTS, HEADS, 3 * HEAD_DIM), 1.0, 6.0, ((0, 16), (1, 32)))
    group_index = with_ends(jax.random.randint(key_list[9], (RESPONSES,), 0, PROM_DEV), jax.random.fold_in(key_list[9], 1), 0, PROM_DEV - 1).astype(jnp.int32)
    lengths = with_ends(jax.random.randint(key_list[10], (RESPONSES,), 1, LEN + 1), jax.random.fold_in(key_list[10], 1), 1, LEN).astype(jnp.int32)
    mixed_grad = centred(key_list[11], (TOKENS, CH), 1.0, 6.0, ((0, 512),))
    expert_index_keys = jax.random.split(jax.random.fold_in(key_list[12], 1), TOKENS // LEN)
    expert_index_turns = jax.random.permutation(jax.random.fold_in(key_list[12], 3), TOKENS // LEN)
    expert_index = jax.vmap(lambda own, number: deal_out(jax.random.fold_in(key_list[12], 2), own, number, LEN, EXPERTS, TOP, CAP, 2))(expert_index_keys, expert_index_turns).reshape((TOKENS, TOP))
    route_gain = jnp.clip(0.1 + 0.9 * jax.random.uniform(key_list[13], (TOKENS, TOP), jnp.float32) ** level_of(key_list[13], (TOKENS, TOP), ((0, 512),), -0.2, 0.2), 0.1, 1.0)
    gate_weight = centred(key_list[14], (EXPERTS, EXP_FF, CH), CH ** -0.5, 0.09375, ((0, 16), (1, 32)))
    up_weight = centred(key_list[15], (EXPERTS, EXP_FF, CH), CH ** -0.5, 0.09375, ((0, 16), (1, 32)))
    down_weight = centred(key_list[16], (EXPERTS, EXP_FF, CH), EXP_FF ** -0.5, 0.21875, ((0, 16), (1, 32)))
    return dict(ssm_input=ssm_input, b_inputs=b_inputs, c_readout=c_readout, step_raw=step_raw, decay_rate=decay_rate, skip_gain=skip_gain, conv_weight=conv_weight, prompt_state=prompt_state, prompt_taps=prompt_taps, group_index=group_index, lengths=lengths, mixed_grad=mixed_grad, expert_index=expert_index, route_gain=route_gain, gate_weight=gate_weight, up_weight=up_weight, down_weight=down_weight)


def mixer(x_rows, b_rows, c_rows, step_raw, decay_rate, skip_gain, conv_weight, state_zero, taps_zero, length):
    steps_n, row_width = x_rows.shape
    head_count, head_size, state_n = state_zero.shape
    taps_n = taps_zero.shape[1] // head_size
    prior = jnp.transpose(taps_zero.reshape(head_count, taps_n, head_size), (1, 0, 2)).reshape(taps_n, row_width)
    series = jnp.concatenate([prior, x_rows.astype(jnp.float32)], 0)
    summed = conv_weight[taps_n] * series[taps_n:]
    for offset in range(taps_n):
        summed = summed + conv_weight[offset] * series[offset:offset + steps_n]
    conv_out = jax.nn.silu(summed).reshape(steps_n, head_count, head_size)
    step_size = jax.nn.softplus(step_raw)
    decay_sum = jnp.cumsum(-step_size * decay_rate[None, :], axis=0)
    scores = jnp.dot(c_rows, b_rows.T, preferred_element_type=jnp.float32)
    positions = lax.iota(jnp.int32, steps_n)
    causal = positions[:, None] >= positions[None, :]
    gaps = decay_sum.T[:, :, None] - decay_sum.T[:, None, :]
    factor = jnp.where(causal[None], jnp.exp(jnp.where(causal[None], gaps, -60.0)), 0.0)
    factor = factor * scores[None] * step_size.T[:, None, :]
    inner = jnp.einsum('hts,shp->thp', factor, conv_out, precision=lax.Precision.HIGHEST)
    carried = jnp.dot(c_rows.astype(jnp.float32), state_zero.reshape(head_count * head_size, state_n).T, precision=lax.Precision.HIGHEST).reshape(steps_n, head_count, head_size)
    output = inner + jnp.exp(decay_sum)[:, :, None] * carried + skip_gain[None, :, None] * conv_out
    live = (positions < length)[:, None, None]
    return jnp.where(live, output, 0.0).reshape(steps_n, row_width)

def expert_apply(total, rows, gate_w, up_w, down_w):
    dims = (((1,), (1,)), ((), ()))
    gate = lax.dot_general(rows, gate_w, dims, preferred_element_type=jnp.float32)
    upper = lax.dot_general(rows, up_w, dims, preferred_element_type=jnp.float32)
    hidden = (jax.nn.silu(gate) * upper).astype(jnp.bfloat16)
    return total + jnp.dot(hidden, down_w, preferred_element_type=jnp.float32)

def reference(ssm_input, b_inputs, c_readout, step_raw, decay_rate, skip_gain, conv_weight, prompt_state, prompt_taps, group_index, lengths, mixed_grad, expert_index, route_gain, gate_weight, up_weight, down_weight):
    resp_n = RESPONSES
    column = lax.iota(jnp.int32, resp_n) % N_EXPERT
    owner = (column * PROM_DEV + group_index).astype(jnp.int32)
    items = (ssm_input.reshape(resp_n, LEN, CH), b_inputs.reshape(resp_n, LEN, STATE), c_readout.reshape(resp_n, LEN, STATE), step_raw.reshape(resp_n, LEN, HEADS), lengths, mixed_grad.reshape(resp_n, LEN, CH), owner)

    def one_response(carry, item):
        acc_state, acc_taps = carry
        x_rows, b_rows, c_rows, raw, length, cotangent, prompt_id = item
        state_zero = lax.dynamic_index_in_dim(prompt_state, prompt_id, 0, keepdims=False).astype(jnp.float32)
        taps_zero = lax.dynamic_index_in_dim(prompt_taps, prompt_id, 0, keepdims=False).astype(jnp.float32)

        def forward(state_in, taps_in):
            return mixer(x_rows, b_rows, c_rows, raw, decay_rate, skip_gain, conv_weight, state_in, taps_in, length)
        mixed, pull = jax.vjp(forward, state_zero, taps_zero)
        grad_s, grad_t = pull(cotangent.astype(jnp.float32))
        grad_s = lax.optimization_barrier(grad_s.astype(jnp.bfloat16)).astype(jnp.float32)
        grad_t = lax.optimization_barrier(grad_t.astype(jnp.bfloat16)).astype(jnp.float32)
        acc_state = acc_state.at[prompt_id].add(grad_s)
        acc_taps = acc_taps.at[prompt_id].add(grad_t)
        return ((acc_state, acc_taps), mixed.astype(jnp.bfloat16))
    start = (jnp.zeros((PROMPTS, HEADS, HEAD_DIM, STATE), jnp.float32), jnp.zeros((PROMPTS, HEADS, 3 * HEAD_DIM), jnp.float32))
    (state_grad, taps_grad), rows = lax.scan(one_response, start, items)
    rows = rows.reshape(TOKENS, CH)
    chosen = expert_index[:, 0].reshape(resp_n, LEN)
    onehot = (chosen[:, :, None] == lax.iota(jnp.int32, EXPERTS)[None, None, :]).astype(jnp.int32)
    slot = lax.optimization_barrier(jnp.sum((jnp.cumsum(onehot, axis=1) - onehot) * onehot, axis=2))
    block = lax.iota(jnp.int32, resp_n)[:, None]
    token_id = lax.iota(jnp.int32, TOKENS).reshape(resp_n, LEN)
    table = jnp.full((EXPERTS, resp_n * CAP), TOKENS, jnp.int32).at[chosen, block * CAP + slot].set(token_id)
    padded = jnp.concatenate([rows, jnp.zeros((1, CH), jnp.bfloat16)], 0)

    def per_expert(result, expert):
        picks = table[expert]
        gathered = padded[picks]
        output = expert_apply(jnp.zeros((picks.shape[0], CH), jnp.float32), gathered, gate_weight[expert], up_weight[expert], down_weight[expert]).astype(jnp.bfloat16)
        return (result.at[picks].set(output), None)
    result, unused = lax.scan(per_expert, jnp.zeros((TOKENS + 1, CH), jnp.bfloat16), lax.iota(jnp.int32, EXPERTS))
    moe_out = (route_gain[:, :1] * result[:TOKENS].astype(jnp.float32)).astype(jnp.bfloat16)
    return (moe_out, state_grad, taps_grad)
```

```python
import functools

import jax
import jax.numpy as jnp
from jax import lax
from jax.experimental import pallas as pl
from jax.experimental.pallas import tpu as pltpu
from jax.sharding import Mesh
from jax.sharding import PartitionSpec as P

AXES = ("y", "xh", "xl", "z", "c")
PLANE = ("y", "xh", "xl")
LINE = ("xh", "z")
GROUPS = 4


def mixer(
    x_rows,
    b_rows,
    c_rows,
    step_raw,
    decay_rate,
    skip_gain,
    conv_weight,
    state_zero,
    taps_zero,
    length,
):
    steps_n, row_width = x_rows.shape
    head_count, head_size, state_n = state_zero.shape
    taps_n = taps_zero.shape[1] // head_size
    prior = jnp.transpose(taps_zero.reshape(head_count, taps_n, head_size), (1, 0, 2)).reshape(
        taps_n, row_width
    )
    series = jnp.concatenate([prior, x_rows.astype(jnp.float32)], 0)
    summed = conv_weight[taps_n] * series[taps_n:]
    for offset in range(taps_n):
        summed = summed + conv_weight[offset] * series[offset : offset + steps_n]
    conv_out = jax.nn.silu(summed).reshape(steps_n, head_count, head_size)
    step_size = jax.nn.softplus(step_raw)
    decay_sum = jnp.cumsum(-step_size * decay_rate[None, :], axis=0)
    scores = jnp.dot(c_rows, b_rows.T, preferred_element_type=jnp.float32)
    positions = lax.iota(jnp.int32, steps_n)
    causal = positions[:, None] >= positions[None, :]
    gaps = decay_sum.T[:, :, None] - decay_sum.T[:, None, :]
    factor = jnp.where(causal[None], jnp.exp(jnp.where(causal[None], gaps, -60.0)), 0.0)
    factor = factor * scores[None] * step_size.T[:, None, :]
    inner = jnp.einsum("hts,shp->thp", factor, conv_out, precision=lax.Precision.HIGHEST)
    carried = jnp.dot(
        c_rows.astype(jnp.float32),
        state_zero.reshape(head_count * head_size, state_n).T,
        precision=lax.Precision.HIGHEST,
    ).reshape(steps_n, head_count, head_size)
    output = inner + jnp.exp(decay_sum)[:, :, None] * carried + skip_gain[None, :, None] * conv_out
    live = (positions < length)[:, None, None]
    return jnp.where(live, output, 0.0).reshape(steps_n, row_width)


def unpack_rows(slots, sources, group):
    count, total = sources * slots, sources * GROUPS * slots
    row = lax.broadcasted_iota(jnp.int32, (count, total), 0)
    col = lax.broadcasted_iota(jnp.int32, (count, total), 1)
    wanted = (row // slots) * (GROUPS * slots) + group * slots + row % slots
    return (col == wanted).astype(jnp.bfloat16)


def expert_kernel(slots, sources, arrived_ref, weight_ref, out_ref, rows_ref, total_ref):
    step = pl.program_id(0)
    width = arrived_ref.shape[1]

    @pl.when(step == 0)
    def _():
        for group in range(GROUPS):
            pick = unpack_rows(slots, sources, group)
            rows_ref[:, group * width : (group + 1) * width] = jnp.dot(
                pick, arrived_ref[...], preferred_element_type=jnp.float32
            ).astype(jnp.bfloat16)
        total_ref[...] = jnp.zeros_like(total_ref)

    dims = (((1,), (1,)), ((), ()))
    rows = rows_ref[...]
    gate = lax.dot_general(rows, weight_ref[0], dims, preferred_element_type=jnp.float32)
    upper = lax.dot_general(rows, weight_ref[1], dims, preferred_element_type=jnp.float32)
    hidden = (jax.nn.silu(gate) * upper).astype(jnp.bfloat16)
    total_ref[...] += jnp.dot(hidden, weight_ref[2], preferred_element_type=jnp.float32)

    @pl.when(step == pl.num_programs(0) - 1)
    def _():
        packed = None
        for group in range(GROUPS):
            part = total_ref[:, group * width : (group + 1) * width].astype(jnp.bfloat16)
            pick = unpack_rows(slots, sources, group)
            term = lax.dot_general(
                pick, part, (((0,), (0,)), ((), ())), preferred_element_type=jnp.float32
            )
            packed = term if packed is None else packed + term
        out_ref[...] = packed.astype(jnp.bfloat16)


def expert_apply(arrived, weights, slots, sources, chunk=256):
    packed_rows, width = arrived.shape
    units, channels = weights.shape[1:]
    count = slots * sources
    return pl.pallas_call(
        functools.partial(expert_kernel, slots, sources),
        grid=(units // chunk,),
        in_specs=[
            pl.BlockSpec((packed_rows, width), lambda i: (0, 0)),
            pl.BlockSpec((3, chunk, channels), lambda i: (0, i, 0)),
        ],
        out_specs=pl.BlockSpec((packed_rows, width), lambda i: (0, 0)),
        out_shape=jax.ShapeDtypeStruct((packed_rows, width), jnp.bfloat16),
        scratch_shapes=[
            pltpu.VMEM((count, channels), jnp.bfloat16),
            pltpu.VMEM((count, channels), jnp.float32),
        ],
        compiler_params=pltpu.CompilerParams(vmem_limit_bytes=48 * 1024 * 1024),
        cost_estimate=pl.CostEstimate(
            flops=6 * count * units * channels,
            bytes_accessed=6 * units * channels + 4 * packed_rows * width,
            transcendentals=count * units,
        ),
    )(arrived, weights)


def shards(
    ssm_input,
    b_inputs,
    c_readout,
    step_raw,
    decay_rate,
    skip_gain,
    conv_weight,
    prompt_state,
    prompt_taps,
    group_index,
    lengths,
    mixed_grad,
    expert_index,
    route_gain,
    gate_weight,
    up_weight,
    down_weight,
):
    steps_n, row_width = ssm_input.shape
    prompts, own_heads, head_size, state_n = prompt_state.shape
    taps_width = prompt_taps.shape[2]
    owners = lax.axis_size(PLANE)
    lines, expert_count = lax.axis_size(LINE), lax.axis_size(("z", "c"))
    heads = owners * own_heads
    state_rows = own_heads * head_size
    taps_rows = own_heads * taps_width // state_n

    stacked = jnp.concatenate([gate_weight, up_weight, down_weight], 0)
    swapped = lax.ppermute(
        stacked, ("xh", "c"), [(a * 2 + b, b * 2 + a) for a in range(2) for b in range(2)]
    )
    weights = lax.all_gather(swapped, ("y", "xl", "c"), axis=1, tiled=True)

    members = lax.all_gather(group_index, PLANE, axis=0, tiled=True)
    held = jnp.concatenate(
        [
            prompt_state.reshape(prompts, state_rows, state_n),
            prompt_taps.reshape(prompts, taps_rows, state_n),
        ],
        1,
    )
    outgoing_state = jnp.where((members == 0)[:, None, None], held[0][None], held[1][None])
    arrived_state = lax.all_to_all(outgoing_state, PLANE, 0, 0, tiled=True)
    state_piece = arrived_state[:, :state_rows].reshape(heads, head_size, state_n)
    taps_piece = arrived_state[:, state_rows:].reshape(heads, taps_width)

    def forward(state_in, taps_in):
        return mixer(
            ssm_input,
            b_inputs,
            c_readout,
            step_raw,
            decay_rate,
            skip_gain,
            conv_weight,
            state_in,
            taps_in,
            lengths[0],
        )

    mixed, pull = jax.vjp(forward, state_piece.astype(jnp.float32), taps_piece.astype(jnp.float32))
    grad_s, grad_t = pull(mixed_grad.astype(jnp.float32))
    outgoing_grad = jnp.concatenate(
        [
            grad_s.astype(jnp.bfloat16).reshape(owners, state_rows, state_n),
            grad_t.astype(jnp.bfloat16).reshape(owners, taps_rows, state_n),
        ],
        1,
    )
    arrived_grad = lax.all_to_all(outgoing_grad, PLANE, 0, 0, tiled=True)
    belongs = (lax.iota(jnp.int32, prompts)[:, None] == members[None, :]).astype(jnp.bfloat16)
    summed = lax.dot_general(
        belongs, arrived_grad, (((1,), (0,)), ((), ())), preferred_element_type=jnp.float32
    )
    state_grad = summed[:, :state_rows].reshape(prompts, own_heads, head_size, state_n)
    taps_grad = summed[:, state_rows:].reshape(prompts, own_heads, taps_width)

    slots = 3 * steps_n // (2 * expert_count)
    width = row_width // GROUPS
    rows = mixed.astype(jnp.bfloat16)
    chosen = expert_index[:, 0]
    onehot = (chosen[:, None] == lax.iota(jnp.int32, expert_count)[None, :]).astype(jnp.int32)
    slot = jnp.sum((jnp.cumsum(onehot, axis=0) - onehot) * onehot, axis=1)
    place = (chosen % 2) * (lines // 2) + chosen // 2
    base = place * (GROUPS * slots) + slot
    packed_rows = lines * GROUPS * slots
    spots = lax.iota(jnp.int32, packed_rows)
    placing = [
        (spots[:, None] == (base + group * slots)[None, :]).astype(jnp.bfloat16)
        for group in range(GROUPS)
    ]
    outgoing = None
    for group in range(GROUPS):
        term = jnp.dot(
            placing[group],
            rows[:, group * width : (group + 1) * width],
            preferred_element_type=jnp.float32,
        )
        outgoing = term if outgoing is None else outgoing + term
    arrived = lax.all_to_all(
        outgoing.astype(jnp.bfloat16).reshape(lines, GROUPS * slots, width), LINE, 0, 0, tiled=True
    )
    produced = expert_apply(arrived.reshape(packed_rows, width), weights, slots, lines)
    returned = lax.all_to_all(
        produced.reshape(lines, GROUPS * slots, width), LINE, 0, 0, tiled=True
    ).reshape(packed_rows, width)
    per_token = jnp.concatenate(
        [
            lax.dot_general(
                placing[group], returned, (((0,), (0,)), ((), ())), preferred_element_type=jnp.float32
            )
            for group in range(GROUPS)
        ],
        1,
    )
    moe_out = (route_gain * per_token).astype(jnp.bfloat16)
    return (moe_out, state_grad, taps_grad)


def solution(mesh):
    prompt, dp, expert = (mesh.shape[name] for name in ("prompt", "dp", "expert"))
    fine = Mesh(mesh.devices.reshape(prompt, 2, dp // 2, expert // 2, 2), AXES)
    tokens = P(AXES, None)
    single = P(AXES)
    experts, plane = ("z", "c"), PLANE
    return jax.shard_map(
        shards,
        mesh=fine,
        in_specs=(
            tokens,
            tokens,
            tokens,
            tokens,
            P(),
            P(),
            P(),
            P(experts, plane, None, None),
            P(experts, plane, None),
            single,
            single,
            tokens,
            tokens,
            tokens,
            P(experts, plane, None),
            P(experts, plane, None),
            P(experts, plane, None),
        ),
        out_specs=(
            tokens,
            P(experts, plane, None, None),
            P(experts, plane, None),
        ),
        check_vma=False,
    )
```

```python
import functools

import jax
import jax.numpy as jnp
from jax import lax
from jax.experimental import pallas as pl
from jax.experimental.pallas import tpu as pltpu
from jax.sharding import Mesh
from jax.sharding import PartitionSpec as P

AXES = ("y", "xh", "xl", "z", "c")
PLANE = ("y", "xh", "xl")
LINE = ("xh", "z")
GROUPS = 4


def spread(values, first, width, head_size):
    heads = values.shape[1]
    head = lax.broadcasted_iota(jnp.int32, (heads, width), 0)
    channel = lax.broadcasted_iota(jnp.int32, (heads, width), 1) + first
    pick = (channel // head_size == head).astype(jnp.float32)
    return jnp.dot(values, pick, precision=lax.Precision.HIGHEST, preferred_element_type=jnp.float32)


def mixer_kernel(
    head_size,
    length_ref,
    x_ref,
    prior_ref,
    conv_ref,
    skip_ref,
    grad_ref,
    b_ref,
    c_ref,
    step_ref,
    rate_ref,
    base_ref,
    state_grad_ref,
    taps_grad_ref,
    grow_ref,
    series_ref,
    scores_ref,
    first_ref,
    decay_ref,
):
    step = pl.program_id(0)
    steps_n, width = x_ref.shape
    exact = dict(precision=lax.Precision.HIGHEST, preferred_element_type=jnp.float32)
    across = (((1,), (1,)), ((), ()))
    down = (((0,), (0,)), ((), ()))

    @pl.when(step == 0)
    def _():
        row = lax.broadcasted_iota(jnp.int32, (steps_n, steps_n), 0)
        col = lax.broadcasted_iota(jnp.int32, (steps_n, steps_n), 1)
        scores = lax.dot_general(
            c_ref[...], b_ref[...], across, preferred_element_type=jnp.float32
        )
        scores_ref[...] = jnp.where(row >= col, scores, 0.0)
        turned = lax.dot_general(
            b_ref[...], c_ref[...], across, preferred_element_type=jnp.float32
        )
        first_ref[...] = jnp.where(col >= row, turned, 0.0)[: first_ref.shape[0]]
        lower = (row >= col).astype(jnp.float32)
        decay_sum = jnp.dot(lower, -step_ref[...] * rate_ref[...], **exact)
        grow_ref[...] = jnp.exp(decay_sum)
        decay_ref[...] = step_ref[...] * jnp.exp(-decay_sum)

    grow = spread(grow_ref[...], step * width, width, head_size)
    shrink = spread(decay_ref[...], step * width, width, head_size)
    series_ref[0:8] = prior_ref[...]
    series_ref[8 : 8 + steps_n] = x_ref[...].astype(jnp.float32)
    taps = [conv_ref[k : k + 1] for k in range(4)]
    summed = taps[3] * series_ref[8 : 8 + steps_n]
    for k in range(3):
        summed = summed + taps[k] * series_ref[5 + k : 5 + k + steps_n]
    conv_out = summed * jax.nn.sigmoid(summed)
    skip = skip_ref[...]
    inner = jnp.dot(scores_ref[...], conv_out * shrink, **exact)
    base_ref[...] = grow * inner + skip * conv_out

    live = lax.broadcasted_iota(jnp.int32, (steps_n, width), 0) < length_ref[0]
    given = jnp.where(live, grad_ref[...].astype(jnp.float32), 0.0)
    scaled = grow * given
    high = scaled.astype(jnp.bfloat16)
    low = (scaled - high.astype(jnp.float32)).astype(jnp.bfloat16)
    c_rows = c_ref[...]
    state_grad_ref[...] = (
        lax.dot_general(high, c_rows, down, preferred_element_type=jnp.float32)
        + lax.dot_general(low, c_rows, down, preferred_element_type=jnp.float32)
    ).astype(jnp.bfloat16)
    early = first_ref.shape[0]
    conv_grad = shrink[:early] * jnp.dot(first_ref[...], scaled, **exact) + skip * given[:early]
    gate = jax.nn.sigmoid(summed[:early])
    series_grad = conv_grad * gate * (1.0 + summed[:early] * (1.0 - gate))
    one, two, three = (series_grad[k : k + 1] for k in range(3))
    taps_grad_ref[...] = jnp.zeros_like(taps_grad_ref)
    taps_grad_ref[0:1] = taps[0] * one
    taps_grad_ref[1:2] = taps[1] * one + taps[0] * two
    taps_grad_ref[2:3] = taps[2] * one + taps[1] * two + taps[0] * three


def mixer_base(
    length, x_rows, prior, conv_weight, skip, grads, b_rows, c_rows, step_size, rate, head_size, block=512
):
    steps_n, channels = x_rows.shape
    heads, state_n = step_size.shape[1], c_rows.shape[1]
    whole = lambda *shape: pl.BlockSpec(shape, lambda i: (0,) * len(shape))
    part = lambda rows: pl.BlockSpec((rows, block), lambda i: (0, i))
    return pl.pallas_call(
        functools.partial(mixer_kernel, head_size),
        grid=(channels // block,),
        in_specs=[
            pl.BlockSpec(memory_space=pltpu.SMEM),
            part(steps_n),
            part(8),
            part(4),
            part(1),
            part(steps_n),
            whole(steps_n, state_n),
            whole(steps_n, state_n),
            whole(steps_n, heads),
            whole(1, heads),
        ],
        out_specs=[
            part(steps_n),
            pl.BlockSpec((block, state_n), lambda i: (i, 0)),
            part(8),
            whole(steps_n, heads),
        ],
        out_shape=[
            jax.ShapeDtypeStruct((steps_n, channels), jnp.float32),
            jax.ShapeDtypeStruct((channels, state_n), jnp.bfloat16),
            jax.ShapeDtypeStruct((8, channels), jnp.float32),
            jax.ShapeDtypeStruct((steps_n, heads), jnp.float32),
        ],
        scratch_shapes=[
            pltpu.VMEM((8 + steps_n, block), jnp.float32),
            pltpu.VMEM((steps_n, steps_n), jnp.float32),
            pltpu.VMEM((8, steps_n), jnp.float32),
            pltpu.VMEM((steps_n, heads), jnp.float32),
        ],
        compiler_params=pltpu.CompilerParams(vmem_limit_bytes=32 * 1024 * 1024),
        cost_estimate=pl.CostEstimate(
            flops=20 * steps_n * channels * state_n,
            bytes_accessed=10 * steps_n * channels,
            transcendentals=steps_n * channels,
        ),
    )(length, x_rows, prior, conv_weight, skip, grads, b_rows, c_rows, step_size, rate)


def dispatch_kernel(
    head_size, slots, length_ref, base_ref, state_ref, c_ref, grow_ref, spot_ref, out_ref, total_ref
):
    group = pl.program_id(0)
    steps_n, width = base_ref.shape
    carried = lax.dot_general(
        c_ref[...], state_ref[...], (((1,), (1,)), ((), ())), preferred_element_type=jnp.float32
    )
    grow = spread(grow_ref[...], group * width, width, head_size)
    live = lax.broadcasted_iota(jnp.int32, (steps_n, width), 0) < length_ref[0]
    rows = jnp.where(live, base_ref[...] + grow * carried, 0.0).astype(jnp.bfloat16)
    packed = out_ref.shape[0]
    spots = lax.broadcasted_iota(jnp.int32, (packed, steps_n), 0)
    placing = (spots == spot_ref[...] + group * slots).astype(jnp.bfloat16)
    term = jnp.dot(placing, rows, preferred_element_type=jnp.float32)

    @pl.when(group == 0)
    def _():
        total_ref[...] = term

    @pl.when(group > 0)
    def _():
        total_ref[...] += term

    @pl.when(group == GROUPS - 1)
    def _():
        out_ref[...] = total_ref[...].astype(jnp.bfloat16)


def dispatch(length, base, state, c_rows, grow, spot, head_size, slots, packed):
    steps_n, channels = base.shape
    state_n, heads, width = state.shape[1], grow.shape[1], channels // GROUPS
    return pl.pallas_call(
        functools.partial(dispatch_kernel, head_size, slots),
        grid=(GROUPS,),
        in_specs=[
            pl.BlockSpec(memory_space=pltpu.SMEM),
            pl.BlockSpec((steps_n, width), lambda g: (0, g)),
            pl.BlockSpec((width, state_n), lambda g: (g, 0)),
            pl.BlockSpec((steps_n, state_n), lambda g: (0, 0)),
            pl.BlockSpec((steps_n, heads), lambda g: (0, 0)),
            pl.BlockSpec((1, steps_n), lambda g: (0, 0)),
        ],
        out_specs=pl.BlockSpec((packed, width), lambda g: (0, 0)),
        out_shape=jax.ShapeDtypeStruct((packed, width), jnp.bfloat16),
        scratch_shapes=[pltpu.VMEM((packed, width), jnp.float32)],
        compiler_params=pltpu.CompilerParams(vmem_limit_bytes=32 * 1024 * 1024),
        cost_estimate=pl.CostEstimate(
            flops=2 * channels * steps_n * (packed + state_n),
            bytes_accessed=6 * channels * steps_n + 2 * packed * width,
            transcendentals=0,
        ),
    )(length, base, state, c_rows, grow, spot)


def unpack_rows(slots, sources, group):
    count, total = sources * slots, sources * GROUPS * slots
    row = lax.broadcasted_iota(jnp.int32, (count, total), 0)
    col = lax.broadcasted_iota(jnp.int32, (count, total), 1)
    wanted = (row // slots) * (GROUPS * slots) + group * slots + row % slots
    return (col == wanted).astype(jnp.bfloat16)


def unpack_kernel(slots, sources, arrived_ref, rows_ref):
    pick = unpack_rows(slots, sources, pl.program_id(0))
    rows_ref[...] = jnp.dot(
        pick, arrived_ref[...], preferred_element_type=jnp.float32
    ).astype(jnp.bfloat16)


def unpack(arrived, slots, sources):
    packed, width = arrived.shape
    count = slots * sources
    return pl.pallas_call(
        functools.partial(unpack_kernel, slots, sources),
        grid=(GROUPS,),
        in_specs=[pl.BlockSpec((packed, width), lambda g: (0, 0))],
        out_specs=pl.BlockSpec((count, width), lambda g: (0, g)),
        out_shape=jax.ShapeDtypeStruct((count, GROUPS * width), jnp.bfloat16),
        compiler_params=pltpu.CompilerParams(vmem_limit_bytes=24 * 1024 * 1024),
        cost_estimate=pl.CostEstimate(
            flops=2 * GROUPS * count * packed * width,
            bytes_accessed=4 * packed * width,
            transcendentals=0,
        ),
    )(arrived)


def expert_kernel(slots, sources, rows_ref, weight_ref, out_ref, total_ref):
    step = pl.program_id(0)
    width = out_ref.shape[1]
    dims = (((1,), (1,)), ((), ()))
    rows = rows_ref[...]
    gate = lax.dot_general(rows, weight_ref[0], dims, preferred_element_type=jnp.float32)
    upper = lax.dot_general(rows, weight_ref[1], dims, preferred_element_type=jnp.float32)
    hidden = (jax.nn.silu(gate) * upper).astype(jnp.bfloat16)
    part = jnp.dot(hidden, weight_ref[2], preferred_element_type=jnp.float32)

    @pl.when(step == 0)
    def _():
        total_ref[...] = part

    @pl.when(step > 0)
    def _():
        total_ref[...] += part

    @pl.when(step == pl.num_programs(0) - 1)
    def _():
        packed = None
        for group in range(GROUPS):
            block = total_ref[:, group * width : (group + 1) * width].astype(jnp.bfloat16)
            pick = unpack_rows(slots, sources, group)
            term = lax.dot_general(
                pick, block, (((0,), (0,)), ((), ())), preferred_element_type=jnp.float32
            )
            packed = term if packed is None else packed + term
        out_ref[...] = packed.astype(jnp.bfloat16)


def expert_apply(rows, weights, slots, sources, chunk=256):
    count, channels = rows.shape
    units = weights.shape[1]
    packed, width = count * GROUPS, channels // GROUPS
    return pl.pallas_call(
        functools.partial(expert_kernel, slots, sources),
        grid=(units // chunk,),
        in_specs=[
            pl.BlockSpec((count, channels), lambda i: (0, 0)),
            pl.BlockSpec((3, chunk, channels), lambda i: (0, i, 0)),
        ],
        out_specs=pl.BlockSpec((packed, width), lambda i: (0, 0)),
        out_shape=jax.ShapeDtypeStruct((packed, width), jnp.bfloat16),
        scratch_shapes=[pltpu.VMEM((count, channels), jnp.float32)],
        compiler_params=pltpu.CompilerParams(vmem_limit_bytes=48 * 1024 * 1024),
        cost_estimate=pl.CostEstimate(
            flops=6 * count * units * channels,
            bytes_accessed=6 * units * channels + 4 * packed * width,
            transcendentals=count * units,
        ),
    )(rows, weights)


def deliver(parts, members):
    y, x = lax.axis_index("y"), lax.axis_index(("xh", "xl"))
    size_y, size_x = parts.shape[:2]
    column = []
    for step in range(size_x):
        piece = lax.dynamic_index_in_dim(parts, (x + step) % size_x, 1, keepdims=False)
        if step:
            piece = lax.ppermute(
                piece, ("xh", "xl"), [(i, (i + step) % size_x) for i in range(size_x)]
            )
        column.append(piece)
    total = None
    for step in range(size_y):
        there = (y + step) % size_y
        piece = jnp.stack(
            [lax.dynamic_index_in_dim(block, there, 0, keepdims=False) for block in column], 0
        )
        if step:
            piece = lax.ppermute(piece, "y", [(i, (i + step) % size_y) for i in range(size_y)])
        for k in range(size_x):
            second = lax.dynamic_index_in_dim(
                members, (y - step) % size_y * size_x + (x - k) % size_x, 0, keepdims=False
            )
            value = piece[k].astype(jnp.float32)
            both = jnp.stack([jnp.where(second, 0.0, value), jnp.where(second, value, 0.0)])
            total = both if total is None else total + both
    return total


def shards(
    ssm_input,
    b_inputs,
    c_readout,
    step_raw,
    decay_rate,
    skip_gain,
    conv_weight,
    prompt_state,
    prompt_taps,
    group_index,
    lengths,
    mixed_grad,
    expert_index,
    route_gain,
    gate_weight,
    up_weight,
    down_weight,
):
    steps_n, row_width = ssm_input.shape
    prompts, own_heads, head_size, state_n = prompt_state.shape
    taps_n, lanes = prompt_taps.shape[2] // head_size, own_heads * head_size
    owners = lax.axis_size(PLANE)
    lines, expert_count = lax.axis_size(LINE), lax.axis_size(("z", "c"))
    state_rows = own_heads * head_size

    stacked = jnp.concatenate([gate_weight, up_weight, down_weight], 0)
    swapped = lax.ppermute(
        stacked, ("xh", "c"), [(a * 2 + b, b * 2 + a) for a in range(2) for b in range(2)]
    )
    weights = lax.all_gather(swapped, ("y", "xl", "c"), axis=1, tiled=True)

    own_taps = jnp.transpose(
        prompt_taps.reshape(prompts, own_heads, taps_n, head_size), (0, 2, 1, 3)
    ).reshape(prompts * taps_n, lanes)
    own_member = jnp.broadcast_to(group_index.astype(jnp.bfloat16)[:, None], (1, lanes))
    notice = jnp.concatenate(
        [own_taps, own_member, jnp.zeros((7 - prompts * taps_n, lanes), jnp.bfloat16)], 0
    )
    notices = lax.all_to_all(
        jnp.broadcast_to(notice[None], (owners,) + notice.shape), PLANE, 0, 0, tiled=True
    )
    members = notices[:, prompts * taps_n, 0] > 0.5
    mine = group_index[0] == 1
    prior = jnp.where(mine, notices[:, taps_n : 2 * taps_n], notices[:, :taps_n])
    prior = jnp.transpose(prior, (1, 0, 2)).reshape(taps_n, row_width).astype(jnp.float32)
    prior = jnp.concatenate([jnp.zeros((8 - taps_n, row_width), jnp.float32), prior], 0)

    held = prompt_state.reshape(prompts, state_rows, state_n)
    outgoing_state = jnp.where(members[:, None, None], held[1][None], held[0][None])
    state = lax.all_to_all(outgoing_state, PLANE, 0, 0, tiled=True).reshape(row_width, state_n)

    step_size = jax.nn.softplus(step_raw)
    base, grad_s, grad_t, grow = mixer_base(
        lengths,
        ssm_input,
        prior,
        conv_weight,
        jnp.repeat(skip_gain, head_size)[None, :],
        mixed_grad,
        b_inputs,
        c_readout,
        step_size,
        decay_rate[None, :],
        head_size,
    )
    outgoing_grad = jnp.concatenate(
        [
            grad_s.reshape(owners, state_rows, state_n),
            jnp.transpose(grad_t[:taps_n].astype(jnp.bfloat16).reshape(taps_n, owners, lanes), (1, 0, 2)),
        ],
        1,
    )
    slots = 3 * steps_n // (2 * expert_count)
    width = row_width // GROUPS
    chosen = expert_index[:, 0]
    order = lax.iota(jnp.int32, steps_n)
    before = (chosen[:, None] == chosen[None, :]) & (order[:, None] < order[None, :])
    slot = jnp.sum(before.astype(jnp.int32), axis=0)
    place = (chosen % 2) * (lines // 2) + chosen // 2
    spot = (place * (GROUPS * slots) + slot)[None, :]
    packed_rows = lines * GROUPS * slots
    outgoing = dispatch(lengths, base, state, c_readout, grow, spot, head_size, slots, packed_rows)
    arrived = lax.all_to_all(
        outgoing.reshape(lines, GROUPS * slots, width), LINE, 0, 0, tiled=True
    )
    expert_rows = unpack(arrived.reshape(packed_rows, width), slots, lines)
    weights, outgoing_grad = lax.optimization_barrier((weights, outgoing_grad))
    produced = expert_apply(expert_rows, weights, slots, lines)
    returned = lax.all_to_all(
        produced.reshape(lines, GROUPS * slots, width), LINE, 0, 0, tiled=True
    ).reshape(packed_rows, width)
    spots = lax.iota(jnp.int32, packed_rows)
    placing = [
        (spots[:, None] == spot + group * slots).astype(jnp.bfloat16) for group in range(GROUPS)
    ]
    per_token = jnp.concatenate(
        [
            lax.dot_general(
                placing[group], returned, (((0,), (0,)), ((), ())), preferred_element_type=jnp.float32
            )
            for group in range(GROUPS)
        ],
        1,
    )
    summed = deliver(
        outgoing_grad.reshape(lax.axis_size("y"), -1, state_rows + taps_n, lanes), members
    )
    state_grad = summed[:, :state_rows].reshape(prompts, own_heads, head_size, state_n)
    taps_grad = jnp.transpose(
        summed[:, state_rows:].reshape(prompts, taps_n, own_heads, head_size), (0, 2, 1, 3)
    ).reshape(prompts, own_heads, taps_n * head_size)
    moe_out = (route_gain * per_token).astype(jnp.bfloat16)
    return (moe_out, state_grad, taps_grad)


def solution(mesh):
    prompt, dp, expert = (mesh.shape[name] for name in ("prompt", "dp", "expert"))
    fine = Mesh(mesh.devices.reshape(prompt, 2, dp // 2, expert // 2, 2), AXES)
    tokens = P(AXES, None)
    single = P(AXES)
    experts, plane = ("z", "c"), PLANE
    return jax.shard_map(
        shards,
        mesh=fine,
        in_specs=(
            tokens,
            tokens,
            tokens,
            tokens,
            P(),
            P(),
            P(),
            P(experts, plane, None, None),
            P(experts, plane, None),
            single,
            single,
            tokens,
            tokens,
            tokens,
            P(experts, plane, None),
            P(experts, plane, None),
            P(experts, plane, None),
        ),
        out_specs=(
            tokens,
            P(experts, plane, None, None),
            P(experts, plane, None),
        ),
        check_vma=False,
    )
```

```python
import functools

import jax
import jax.numpy as jnp
from jax import lax
from jax.experimental import pallas as pl
from jax.experimental.pallas import tpu as pltpu
from jax.sharding import Mesh
from jax.sharding import PartitionSpec as P

AXES = ("y", "xh", "xl", "z", "c")
PLANE = ("y", "xh", "xl")
LINE = ("xh", "z")
GROUPS = 4


def spread(values, first, width, head_size):
    heads = values.shape[1]
    head = lax.broadcasted_iota(jnp.int32, (heads, width), 0)
    channel = lax.broadcasted_iota(jnp.int32, (heads, width), 1) + first
    pick = (channel // head_size == head).astype(jnp.float32)
    return jnp.dot(values, pick, precision=lax.Precision.HIGHEST, preferred_element_type=jnp.float32)


def mixer_kernel(
    head_size,
    length_ref,
    row_ref,
    x_ref,
    prior_ref,
    conv_ref,
    skip_ref,
    grad_ref,
    b_ref,
    c_ref,
    step_ref,
    rate_ref,
    base_ref,
    sent_ref,
    grow_ref,
    series_ref,
    scores_ref,
    first_ref,
    decay_ref,
):
    step = pl.program_id(0)
    steps_n, width = x_ref.shape
    exact = dict(precision=lax.Precision.HIGHEST, preferred_element_type=jnp.float32)
    across = (((1,), (1,)), ((), ()))
    down = (((0,), (0,)), ((), ()))

    @pl.when(step == 0)
    def _():
        row = lax.broadcasted_iota(jnp.int32, (steps_n, steps_n), 0)
        col = lax.broadcasted_iota(jnp.int32, (steps_n, steps_n), 1)
        scores = lax.dot_general(
            c_ref[...], b_ref[...], across, preferred_element_type=jnp.float32
        )
        scores_ref[...] = jnp.where(row >= col, scores, 0.0)
        turned = lax.dot_general(
            b_ref[...], c_ref[...], across, preferred_element_type=jnp.float32
        )
        first_ref[...] = jnp.where(col >= row, turned, 0.0)[: first_ref.shape[0]]
        lower = (row >= col).astype(jnp.float32)
        decay_sum = jnp.dot(lower, -step_ref[...] * rate_ref[...], **exact)
        grow_ref[...] = jnp.exp(decay_sum)
        decay_ref[...] = step_ref[...] * jnp.exp(-decay_sum)

    grow = spread(grow_ref[...], step * width, width, head_size)
    shrink = spread(decay_ref[...], step * width, width, head_size)
    series_ref[0:8] = prior_ref[...]
    series_ref[8 : 8 + steps_n] = x_ref[...].astype(jnp.float32)
    taps = [conv_ref[k : k + 1] for k in range(4)]
    summed = taps[3] * series_ref[8 : 8 + steps_n]
    for k in range(3):
        summed = summed + taps[k] * series_ref[5 + k : 5 + k + steps_n]
    conv_out = summed * jax.nn.sigmoid(summed)
    skip = skip_ref[...]
    inner = jnp.dot(scores_ref[...], conv_out * shrink, **exact)
    base_ref[...] = grow * inner + skip * conv_out

    live = lax.broadcasted_iota(jnp.int32, (steps_n, width), 0) < length_ref[0]
    given = jnp.where(live, grad_ref[...].astype(jnp.float32), 0.0)
    scaled = grow * given
    high = scaled.astype(jnp.bfloat16)
    low = (scaled - high.astype(jnp.float32)).astype(jnp.bfloat16)
    c_rows = c_ref[...]
    state_grad = (
        lax.dot_general(high, c_rows, down, preferred_element_type=jnp.float32)
        + lax.dot_general(low, c_rows, down, preferred_element_type=jnp.float32)
    ).astype(jnp.bfloat16)
    early = first_ref.shape[0]
    conv_grad = shrink[:early] * jnp.dot(first_ref[...], scaled, **exact) + skip * given[:early]
    gate = jax.nn.sigmoid(summed[:early])
    series_grad = conv_grad * gate * (1.0 + summed[:early] * (1.0 - gate))
    one, two, three = (series_grad[k : k + 1] for k in range(3))
    places = sent_ref.shape[0]
    lanes = width // places
    taps_rows = sent_ref.shape[2] - lanes
    taps_grad = jnp.concatenate(
        [
            taps[0] * one,
            taps[1] * one + taps[0] * two,
            taps[2] * one + taps[1] * two + taps[0] * three,
            jnp.zeros((taps_rows - 3, width), jnp.float32),
        ],
        0,
    ).astype(jnp.bfloat16)
    for k in range(places):
        sent_ref[k, 0, :lanes] = state_grad[k * lanes : (k + 1) * lanes]
        sent_ref[k, 0, lanes:] = taps_grad[:, k * lanes : (k + 1) * lanes]


def mixer_base(
    length, row, x_rows, prior, conv_weight, skip, grads, b_rows, c_rows, step_size, rate, head_size, owners
):
    steps_n, channels = x_rows.shape
    heads, state_n = step_size.shape[1], c_rows.shape[1]
    owners_y, owners_x = owners
    lanes = channels // (owners_y * owners_x)
    block = owners_x * lanes
    whole = lambda *shape: pl.BlockSpec(shape, lambda i, *_: (0,) * len(shape))
    part = lambda rows: pl.BlockSpec((rows, block), lambda i, *_: (0, i))
    sent = (owners_x, owners_y, lanes + 16, state_n)
    return pl.pallas_call(
        functools.partial(mixer_kernel, head_size),
        grid_spec=pltpu.PrefetchScalarGridSpec(
            num_scalar_prefetch=2,
            grid=(owners_y,),
            in_specs=[
                part(steps_n),
                part(8),
                part(4),
                part(1),
                part(steps_n),
                whole(steps_n, state_n),
                whole(steps_n, state_n),
                whole(steps_n, heads),
                whole(1, heads),
            ],
            out_specs=[
                part(steps_n),
                pl.BlockSpec(
                    (owners_x, 1, lanes + 16, state_n),
                    lambda i, _, row_ref: (0, lax.rem(i - row_ref[0] + owners_y, owners_y), 0, 0),
                ),
                whole(steps_n, heads),
            ],
            scratch_shapes=[
                pltpu.VMEM((8 + steps_n, block), jnp.float32),
                pltpu.VMEM((steps_n, steps_n), jnp.float32),
                pltpu.VMEM((8, steps_n), jnp.float32),
                pltpu.VMEM((steps_n, heads), jnp.float32),
            ],
        ),
        out_shape=[
            jax.ShapeDtypeStruct((steps_n, channels), jnp.float32),
            jax.ShapeDtypeStruct(sent, jnp.bfloat16),
            jax.ShapeDtypeStruct((steps_n, heads), jnp.float32),
        ],
        compiler_params=pltpu.CompilerParams(vmem_limit_bytes=32 * 1024 * 1024),
        cost_estimate=pl.CostEstimate(
            flops=20 * steps_n * channels * state_n,
            bytes_accessed=10 * steps_n * channels,
            transcendentals=steps_n * channels,
        ),
    )(length, row, x_rows, prior, conv_weight, skip, grads, b_rows, c_rows, step_size, rate)


def dispatch_kernel(
    head_size, slots, length_ref, base_ref, state_ref, c_ref, grow_ref, spot_ref, out_ref, total_ref
):
    group = pl.program_id(0)
    steps_n, width = base_ref.shape
    carried = lax.dot_general(
        c_ref[...], state_ref[...], (((1,), (1,)), ((), ())), preferred_element_type=jnp.float32
    )
    grow = spread(grow_ref[...], group * width, width, head_size)
    live = lax.broadcasted_iota(jnp.int32, (steps_n, width), 0) < length_ref[0]
    rows = jnp.where(live, base_ref[...] + grow * carried, 0.0).astype(jnp.bfloat16)
    packed = out_ref.shape[0]
    spots = lax.broadcasted_iota(jnp.int32, (packed, steps_n), 0)
    placing = (spots == spot_ref[...] + group * slots).astype(jnp.bfloat16)
    term = jnp.dot(placing, rows, preferred_element_type=jnp.float32)

    @pl.when(group == 0)
    def _():
        total_ref[...] = term

    @pl.when(group > 0)
    def _():
        total_ref[...] += term

    @pl.when(group == GROUPS - 1)
    def _():
        out_ref[...] = total_ref[...].astype(jnp.bfloat16)


def dispatch(length, base, state, c_rows, grow, spot, head_size, slots, packed):
    steps_n, channels = base.shape
    state_n, heads, width = state.shape[1], grow.shape[1], channels // GROUPS
    return pl.pallas_call(
        functools.partial(dispatch_kernel, head_size, slots),
        grid=(GROUPS,),
        in_specs=[
            pl.BlockSpec(memory_space=pltpu.SMEM),
            pl.BlockSpec((steps_n, width), lambda g: (0, g)),
            pl.BlockSpec((width, state_n), lambda g: (g, 0)),
            pl.BlockSpec((steps_n, state_n), lambda g: (0, 0)),
            pl.BlockSpec((steps_n, heads), lambda g: (0, 0)),
            pl.BlockSpec((1, steps_n), lambda g: (0, 0)),
        ],
        out_specs=pl.BlockSpec((packed, width), lambda g: (0, 0)),
        out_shape=jax.ShapeDtypeStruct((packed, width), jnp.bfloat16),
        scratch_shapes=[pltpu.VMEM((packed, width), jnp.float32)],
        compiler_params=pltpu.CompilerParams(vmem_limit_bytes=32 * 1024 * 1024),
        cost_estimate=pl.CostEstimate(
            flops=2 * channels * steps_n * (packed + state_n),
            bytes_accessed=6 * channels * steps_n + 2 * packed * width,
            transcendentals=0,
        ),
    )(length, base, state, c_rows, grow, spot)


def unpack_rows(slots, sources, group):
    count, total = sources * slots, sources * GROUPS * slots
    row = lax.broadcasted_iota(jnp.int32, (count, total), 0)
    col = lax.broadcasted_iota(jnp.int32, (count, total), 1)
    wanted = (row // slots) * (GROUPS * slots) + group * slots + row % slots
    return (col == wanted).astype(jnp.bfloat16)


def unpack_kernel(slots, sources, arrived_ref, rows_ref):
    pick = unpack_rows(slots, sources, pl.program_id(0))
    rows_ref[...] = jnp.dot(
        pick, arrived_ref[...], preferred_element_type=jnp.float32
    ).astype(jnp.bfloat16)


def unpack(arrived, slots, sources):
    packed, width = arrived.shape
    count = slots * sources
    return pl.pallas_call(
        functools.partial(unpack_kernel, slots, sources),
        grid=(GROUPS,),
        in_specs=[pl.BlockSpec((packed, width), lambda g: (0, 0))],
        out_specs=pl.BlockSpec((count, width), lambda g: (0, g)),
        out_shape=jax.ShapeDtypeStruct((count, GROUPS * width), jnp.bfloat16),
        compiler_params=pltpu.CompilerParams(vmem_limit_bytes=24 * 1024 * 1024),
        cost_estimate=pl.CostEstimate(
            flops=2 * GROUPS * count * packed * width,
            bytes_accessed=4 * packed * width,
            transcendentals=0,
        ),
    )(arrived)


def expert_kernel(slots, sources, rows_ref, weight_ref, out_ref, total_ref):
    step = pl.program_id(0)
    width = out_ref.shape[1]
    dims = (((1,), (1,)), ((), ()))
    rows = rows_ref[...]
    gate = lax.dot_general(rows, weight_ref[0], dims, preferred_element_type=jnp.float32)
    upper = lax.dot_general(rows, weight_ref[1], dims, preferred_element_type=jnp.float32)
    hidden = (jax.nn.silu(gate) * upper).astype(jnp.bfloat16)
    part = jnp.dot(hidden, weight_ref[2], preferred_element_type=jnp.float32)

    @pl.when(step == 0)
    def _():
        total_ref[...] = part

    @pl.when(step > 0)
    def _():
        total_ref[...] += part

    @pl.when(step == pl.num_programs(0) - 1)
    def _():
        packed = None
        for group in range(GROUPS):
            block = total_ref[:, group * width : (group + 1) * width].astype(jnp.bfloat16)
            pick = unpack_rows(slots, sources, group)
            term = lax.dot_general(
                pick, block, (((0,), (0,)), ((), ())), preferred_element_type=jnp.float32
            )
            packed = term if packed is None else packed + term
        out_ref[...] = packed.astype(jnp.bfloat16)


def expert_apply(rows, weights, slots, sources, chunk=256):
    count, channels = rows.shape
    units = weights.shape[1]
    packed, width = count * GROUPS, channels // GROUPS
    return pl.pallas_call(
        functools.partial(expert_kernel, slots, sources),
        grid=(units // chunk,),
        in_specs=[
            pl.BlockSpec((count, channels), lambda i: (0, 0)),
            pl.BlockSpec((3, chunk, channels), lambda i: (0, i, 0)),
        ],
        out_specs=pl.BlockSpec((packed, width), lambda i: (0, 0)),
        out_shape=jax.ShapeDtypeStruct((packed, width), jnp.bfloat16),
        scratch_shapes=[pltpu.VMEM((count, channels), jnp.float32)],
        compiler_params=pltpu.CompilerParams(vmem_limit_bytes=48 * 1024 * 1024),
        cost_estimate=pl.CostEstimate(
            flops=6 * count * units * channels,
            bytes_accessed=6 * units * channels + 4 * packed * width,
            transcendentals=count * units,
        ),
    )(rows, weights)


def collect_kernel(row_ref, members_ref, *refs):
    pieces, state_ref, taps_ref, total_ref = refs[:-3], *refs[-3:]
    size_y, size_x = len(pieces), pieces[0].shape[0]
    lanes = state_ref.shape[1]
    total_ref[...] = jnp.zeros_like(total_ref)
    for step in range(size_y):
        source = lax.rem(row_ref[0] - step + size_y, size_y)
        for k in range(size_x):
            member = members_ref[source * size_x + k]
            total_ref[member] += pieces[step][k].astype(jnp.float32)
    state_ref[...] = total_ref[:, :lanes]
    taps_ref[...] = total_ref[:, lanes:]


def collect(row, members, pieces, prompts):
    size_x, rows, lanes = pieces[0].shape
    vmem, smem = pl.BlockSpec(memory_space=pltpu.VMEM), pl.BlockSpec(memory_space=pltpu.SMEM)
    return pl.pallas_call(
        collect_kernel,
        in_specs=[smem, smem] + [vmem] * len(pieces),
        out_specs=[vmem, vmem],
        out_shape=[
            jax.ShapeDtypeStruct((prompts, rows - 16, lanes), jnp.float32),
            jax.ShapeDtypeStruct((prompts, 16, lanes), jnp.float32),
        ],
        scratch_shapes=[pltpu.VMEM((prompts, rows, lanes), jnp.float32)],
        compiler_params=pltpu.CompilerParams(vmem_limit_bytes=16 * 1024 * 1024),
        cost_estimate=pl.CostEstimate(
            flops=len(pieces) * size_x * rows * lanes,
            bytes_accessed=2 * len(pieces) * size_x * rows * lanes,
            transcendentals=0,
        ),
    )(row, members, *pieces)


def shards(
    ssm_input,
    b_inputs,
    c_readout,
    step_raw,
    decay_rate,
    skip_gain,
    conv_weight,
    prompt_state,
    prompt_taps,
    group_index,
    lengths,
    mixed_grad,
    expert_index,
    route_gain,
    gate_weight,
    up_weight,
    down_weight,
):
    steps_n, row_width = ssm_input.shape
    prompts, own_heads, head_size, state_n = prompt_state.shape
    taps_n, lanes = prompt_taps.shape[2] // head_size, own_heads * head_size
    owners = lax.axis_size(PLANE)
    lines, expert_count = lax.axis_size(LINE), lax.axis_size(("z", "c"))
    state_rows = own_heads * head_size

    stacked = jnp.concatenate([gate_weight, up_weight, down_weight], 0)
    swapped = lax.ppermute(
        stacked, ("xh", "c"), [(a * 2 + b, b * 2 + a) for a in range(2) for b in range(2)]
    )
    weights = lax.all_gather(swapped, ("y", "xl", "c"), axis=1, tiled=True)

    row = lax.axis_index("y").astype(jnp.int32)[None]

    own_taps = jnp.transpose(
        prompt_taps.reshape(prompts, own_heads, taps_n, head_size), (0, 2, 1, 3)
    ).reshape(prompts * taps_n, lanes)
    own_member = jnp.broadcast_to(group_index.astype(jnp.bfloat16)[:, None], (1, lanes))
    notice = jnp.concatenate(
        [own_taps, own_member, jnp.zeros((7 - prompts * taps_n, lanes), jnp.bfloat16)], 0
    )
    notices = lax.all_to_all(
        jnp.broadcast_to(notice[None], (owners,) + notice.shape), PLANE, 0, 0, tiled=True
    )
    members = notices[:, prompts * taps_n, 0] > 0.5
    mine = group_index[0] == 1
    prior = jnp.where(mine, notices[:, taps_n : 2 * taps_n], notices[:, :taps_n])
    prior = jnp.transpose(prior, (1, 0, 2)).reshape(taps_n, row_width).astype(jnp.float32)
    prior = jnp.concatenate([jnp.zeros((8 - taps_n, row_width), jnp.float32), prior], 0)

    held = prompt_state.reshape(prompts, state_rows, state_n)
    outgoing_state = jnp.where(members[:, None, None], held[1][None], held[0][None])
    state = lax.all_to_all(outgoing_state, PLANE, 0, 0, tiled=True).reshape(row_width, state_n)

    step_size = jax.nn.softplus(step_raw)
    base, outgoing_grad, grow = mixer_base(
        lengths,
        row,
        ssm_input,
        prior,
        conv_weight,
        jnp.repeat(skip_gain, head_size)[None, :],
        mixed_grad,
        b_inputs,
        c_readout,
        step_size,
        decay_rate[None, :],
        head_size,
        (lax.axis_size("y"), lax.axis_size(("xh", "xl"))),
    )
    column_grad = lax.all_to_all(outgoing_grad, ("xh", "xl"), 0, 0, tiled=True)

    slots = 3 * steps_n // (2 * expert_count)
    width = row_width // GROUPS
    chosen = expert_index[:, 0]
    order = lax.iota(jnp.int32, steps_n)
    before = (chosen[:, None] == chosen[None, :]) & (order[:, None] < order[None, :])
    slot = jnp.sum(before.astype(jnp.int32), axis=0)
    place = (chosen % 2) * (lines // 2) + chosen // 2
    spot = (place * (GROUPS * slots) + slot)[None, :]
    packed_rows = lines * GROUPS * slots
    outgoing = dispatch(lengths, base, state, c_readout, grow, spot, head_size, slots, packed_rows)
    arrived = lax.all_to_all(
        outgoing.reshape(lines, GROUPS * slots, width), LINE, 0, 0, tiled=True
    )
    expert_rows = unpack(arrived.reshape(packed_rows, width), slots, lines)
    produced = expert_apply(expert_rows, weights, slots, lines)
    produced, column_grad = lax.optimization_barrier((produced, column_grad))
    returned = lax.all_to_all(
        produced.reshape(lines, GROUPS * slots, width), LINE, 0, 0, tiled=True
    ).reshape(packed_rows, width)
    spots = lax.iota(jnp.int32, packed_rows)
    placing = [
        (spots[:, None] == spot + group * slots).astype(jnp.bfloat16) for group in range(GROUPS)
    ]
    per_token = jnp.concatenate(
        [
            lax.dot_general(
                placing[group], returned, (((0,), (0,)), ((), ())), preferred_element_type=jnp.float32
            )
            for group in range(GROUPS)
        ],
        1,
    )
    size_y = lax.axis_size("y")
    pieces = [column_grad[:, 0]] + [
        lax.ppermute(column_grad[:, d], "y", [(i, (i + d) % size_y) for i in range(size_y)])
        for d in range(1, size_y)
    ]
    state_sum, taps_sum = collect(row, members.astype(jnp.int32), pieces, prompts)
    state_grad = state_sum.reshape(prompts, own_heads, head_size, state_n)
    taps_grad = jnp.transpose(
        taps_sum[:, :taps_n].reshape(prompts, taps_n, own_heads, head_size), (0, 2, 1, 3)
    ).reshape(prompts, own_heads, taps_n * head_size)
    moe_out = (route_gain * per_token).astype(jnp.bfloat16)
    return (moe_out, state_grad, taps_grad)


def solution(mesh):
    prompt, dp, expert = (mesh.shape[name] for name in ("prompt", "dp", "expert"))
    fine = Mesh(mesh.devices.reshape(prompt, 2, dp // 2, expert // 2, 2), AXES)
    tokens = P(AXES, None)
    single = P(AXES)
    experts, plane = ("z", "c"), PLANE
    return jax.shard_map(
        shards,
        mesh=fine,
        in_specs=(
            tokens,
            tokens,
            tokens,
            tokens,
            P(),
            P(),
            P(),
            P(experts, plane, None, None),
            P(experts, plane, None),
            single,
            single,
            tokens,
            tokens,
            tokens,
            P(experts, plane, None),
            P(experts, plane, None),
            P(experts, plane, None),
        ),
        out_specs=(
            tokens,
            P(experts, plane, None, None),
            P(experts, plane, None),
        ),
        check_vma=False,
    )
```

```python
import functools

import jax
import jax.numpy as jnp
from jax import lax
from jax.experimental import pallas as pl
from jax.experimental.pallas import tpu as pltpu
from jax.sharding import Mesh
from jax.sharding import PartitionSpec as P

AXES = ("y", "xh", "xl", "z", "c")
PLANE = ("y", "xh", "xl")
LINE = ("xh", "xl", "z")
GROUPS = 4


def spread(values, first, width, head_size):
    heads = values.shape[1]
    head = lax.broadcasted_iota(jnp.int32, (heads, width), 0)
    channel = lax.broadcasted_iota(jnp.int32, (heads, width), 1) + first
    pick = (channel // head_size == head).astype(jnp.float32)
    return jnp.dot(values, pick, precision=lax.Precision.HIGHEST, preferred_element_type=jnp.float32)


def mixer_kernel(
    head_size,
    length_ref,
    row_ref,
    x_ref,
    prior_ref,
    conv_ref,
    skip_ref,
    grad_ref,
    b_ref,
    c_ref,
    step_ref,
    rate_ref,
    base_ref,
    sent_ref,
    grow_ref,
    series_ref,
    scores_ref,
    first_ref,
    decay_ref,
):
    step = pl.program_id(0)
    steps_n, width = x_ref.shape
    exact = dict(precision=lax.Precision.HIGHEST, preferred_element_type=jnp.float32)
    across = (((1,), (1,)), ((), ()))
    down = (((0,), (0,)), ((), ()))

    @pl.when(step == 0)
    def _():
        row = lax.broadcasted_iota(jnp.int32, (steps_n, steps_n), 0)
        col = lax.broadcasted_iota(jnp.int32, (steps_n, steps_n), 1)
        scores = lax.dot_general(
            c_ref[...], b_ref[...], across, preferred_element_type=jnp.float32
        )
        scores_ref[...] = jnp.where(row >= col, scores, 0.0)
        turned = lax.dot_general(
            b_ref[...], c_ref[...], across, preferred_element_type=jnp.float32
        )
        first_ref[...] = jnp.where(col >= row, turned, 0.0)[: first_ref.shape[0]]
        lower = (row >= col).astype(jnp.float32)
        decay_sum = jnp.dot(lower, -step_ref[...] * rate_ref[...], **exact)
        grow_ref[...] = jnp.exp(decay_sum)
        decay_ref[...] = step_ref[...] * jnp.exp(-decay_sum)

    grow = spread(grow_ref[...], step * width, width, head_size)
    shrink = spread(decay_ref[...], step * width, width, head_size)
    series_ref[0:8] = prior_ref[...]
    series_ref[8 : 8 + steps_n] = x_ref[...].astype(jnp.float32)
    taps = [conv_ref[k : k + 1] for k in range(4)]
    summed = taps[3] * series_ref[8 : 8 + steps_n]
    for k in range(3):
        summed = summed + taps[k] * series_ref[5 + k : 5 + k + steps_n]
    conv_out = summed * jax.nn.sigmoid(summed)
    skip = skip_ref[...]
    inner = jnp.dot(scores_ref[...], conv_out * shrink, **exact)
    base_ref[...] = grow * inner + skip * conv_out

    live = lax.broadcasted_iota(jnp.int32, (steps_n, width), 0) < length_ref[0]
    given = jnp.where(live, grad_ref[...].astype(jnp.float32), 0.0)
    scaled = grow * given
    high = scaled.astype(jnp.bfloat16)
    low = (scaled - high.astype(jnp.float32)).astype(jnp.bfloat16)
    c_rows = c_ref[...]
    state_grad = (
        lax.dot_general(high, c_rows, down, preferred_element_type=jnp.float32)
        + lax.dot_general(low, c_rows, down, preferred_element_type=jnp.float32)
    ).astype(jnp.bfloat16)
    early = first_ref.shape[0]
    conv_grad = shrink[:early] * jnp.dot(first_ref[...], scaled, **exact) + skip * given[:early]
    gate = jax.nn.sigmoid(summed[:early])
    series_grad = conv_grad * gate * (1.0 + summed[:early] * (1.0 - gate))
    one, two, three = (series_grad[k : k + 1] for k in range(3))
    places = sent_ref.shape[0]
    lanes = width // places
    taps_rows = sent_ref.shape[2] - lanes
    taps_grad = jnp.concatenate(
        [
            taps[0] * one,
            taps[1] * one + taps[0] * two,
            taps[2] * one + taps[1] * two + taps[0] * three,
            jnp.zeros((taps_rows - 3, width), jnp.float32),
        ],
        0,
    ).astype(jnp.bfloat16)
    for k in range(places):
        sent_ref[k, 0, :lanes] = state_grad[k * lanes : (k + 1) * lanes]
        sent_ref[k, 0, lanes:] = taps_grad[:, k * lanes : (k + 1) * lanes]


def mixer_base(
    length, row, x_rows, prior, conv_weight, skip, grads, b_rows, c_rows, step_size, rate, head_size, owners
):
    steps_n, channels = x_rows.shape
    heads, state_n = step_size.shape[1], c_rows.shape[1]
    owners_y, owners_x = owners
    lanes = channels // (owners_y * owners_x)
    block = owners_x * lanes
    whole = lambda *shape: pl.BlockSpec(shape, lambda i, *_: (0,) * len(shape))
    part = lambda rows: pl.BlockSpec((rows, block), lambda i, *_: (0, i))
    sent = (owners_x, owners_y, lanes + 16, state_n)
    return pl.pallas_call(
        functools.partial(mixer_kernel, head_size),
        grid_spec=pltpu.PrefetchScalarGridSpec(
            num_scalar_prefetch=2,
            grid=(owners_y,),
            in_specs=[
                part(steps_n),
                part(8),
                part(4),
                part(1),
                part(steps_n),
                whole(steps_n, state_n),
                whole(steps_n, state_n),
                whole(steps_n, heads),
                whole(1, heads),
            ],
            out_specs=[
                part(steps_n),
                pl.BlockSpec(
                    (owners_x, 1, lanes + 16, state_n),
                    lambda i, _, row_ref: (0, lax.rem(i - row_ref[0] + owners_y, owners_y), 0, 0),
                ),
                whole(steps_n, heads),
            ],
            scratch_shapes=[
                pltpu.VMEM((8 + steps_n, block), jnp.float32),
                pltpu.VMEM((steps_n, steps_n), jnp.float32),
                pltpu.VMEM((8, steps_n), jnp.float32),
                pltpu.VMEM((steps_n, heads), jnp.float32),
            ],
        ),
        out_shape=[
            jax.ShapeDtypeStruct((steps_n, channels), jnp.float32),
            jax.ShapeDtypeStruct(sent, jnp.bfloat16),
            jax.ShapeDtypeStruct((steps_n, heads), jnp.float32),
        ],
        compiler_params=pltpu.CompilerParams(vmem_limit_bytes=32 * 1024 * 1024),
        cost_estimate=pl.CostEstimate(
            flops=20 * steps_n * channels * state_n,
            bytes_accessed=10 * steps_n * channels,
            transcendentals=steps_n * channels,
        ),
    )(length, row, x_rows, prior, conv_weight, skip, grads, b_rows, c_rows, step_size, rate)


def dispatch_kernel(
    head_size, slots, length_ref, base_ref, state_ref, c_ref, grow_ref, spot_ref, out_ref, total_ref
):
    group = pl.program_id(0)
    steps_n, width = base_ref.shape
    carried = lax.dot_general(
        c_ref[...], state_ref[...], (((1,), (1,)), ((), ())), preferred_element_type=jnp.float32
    )
    grow = spread(grow_ref[...], group * width, width, head_size)
    live = lax.broadcasted_iota(jnp.int32, (steps_n, width), 0) < length_ref[0]
    rows = jnp.where(live, base_ref[...] + grow * carried, 0.0).astype(jnp.bfloat16)
    packed = out_ref.shape[0]
    spots = lax.broadcasted_iota(jnp.int32, (packed, steps_n), 0)
    placing = (spots == spot_ref[...] + group * slots).astype(jnp.bfloat16)
    term = jnp.dot(placing, rows, preferred_element_type=jnp.float32)

    @pl.when(group == 0)
    def _():
        total_ref[...] = term

    @pl.when(group > 0)
    def _():
        total_ref[...] += term

    @pl.when(group == GROUPS - 1)
    def _():
        out_ref[...] = total_ref[...].astype(jnp.bfloat16)


def dispatch(length, base, state, c_rows, grow, spot, head_size, slots, packed):
    steps_n, channels = base.shape
    state_n, heads, width = state.shape[1], grow.shape[1], channels // GROUPS
    return pl.pallas_call(
        functools.partial(dispatch_kernel, head_size, slots),
        grid=(GROUPS,),
        in_specs=[
            pl.BlockSpec(memory_space=pltpu.SMEM),
            pl.BlockSpec((steps_n, width), lambda g: (0, g)),
            pl.BlockSpec((width, state_n), lambda g: (g, 0)),
            pl.BlockSpec((steps_n, state_n), lambda g: (0, 0)),
            pl.BlockSpec((steps_n, heads), lambda g: (0, 0)),
            pl.BlockSpec((1, steps_n), lambda g: (0, 0)),
        ],
        out_specs=pl.BlockSpec((packed, width), lambda g: (0, 0)),
        out_shape=jax.ShapeDtypeStruct((packed, width), jnp.bfloat16),
        scratch_shapes=[pltpu.VMEM((packed, width), jnp.float32)],
        compiler_params=pltpu.CompilerParams(vmem_limit_bytes=32 * 1024 * 1024),
        cost_estimate=pl.CostEstimate(
            flops=2 * channels * steps_n * (packed + state_n),
            bytes_accessed=6 * channels * steps_n + 2 * packed * width,
            transcendentals=0,
        ),
    )(length, base, state, c_rows, grow, spot)


def unpack_rows(slots, sources, group):
    count, total = sources * slots, sources * GROUPS * slots
    row = lax.broadcasted_iota(jnp.int32, (count, total), 0)
    col = lax.broadcasted_iota(jnp.int32, (count, total), 1)
    wanted = (row // slots) * (GROUPS * slots) + group * slots + row % slots
    return (col == wanted).astype(jnp.bfloat16)


def unpack_kernel(slots, sources, arrived_ref, rows_ref):
    pick = unpack_rows(slots, sources, pl.program_id(0))
    rows_ref[...] = jnp.dot(
        pick, arrived_ref[...], preferred_element_type=jnp.float32
    ).astype(jnp.bfloat16)


def unpack(arrived, slots, sources):
    packed, width = arrived.shape
    count = slots * sources
    return pl.pallas_call(
        functools.partial(unpack_kernel, slots, sources),
        grid=(GROUPS,),
        in_specs=[pl.BlockSpec((packed, width), lambda g: (0, 0))],
        out_specs=pl.BlockSpec((count, width), lambda g: (0, g)),
        out_shape=jax.ShapeDtypeStruct((count, GROUPS * width), jnp.bfloat16),
        compiler_params=pltpu.CompilerParams(vmem_limit_bytes=24 * 1024 * 1024),
        cost_estimate=pl.CostEstimate(
            flops=2 * GROUPS * count * packed * width,
            bytes_accessed=4 * packed * width,
            transcendentals=0,
        ),
    )(arrived)


def expert_kernel(slots, sources, rows_ref, weight_ref, out_ref, total_ref):
    step = pl.program_id(0)
    width = out_ref.shape[1]
    dims = (((1,), (1,)), ((), ()))
    rows = rows_ref[...]
    gate = lax.dot_general(rows, weight_ref[0], dims, preferred_element_type=jnp.float32)
    upper = lax.dot_general(rows, weight_ref[1], dims, preferred_element_type=jnp.float32)
    hidden = (jax.nn.silu(gate) * upper).astype(jnp.bfloat16)
    part = jnp.dot(hidden, weight_ref[2], preferred_element_type=jnp.float32)

    @pl.when(step == 0)
    def _():
        total_ref[...] = part

    @pl.when(step > 0)
    def _():
        total_ref[...] += part

    @pl.when(step == pl.num_programs(0) - 1)
    def _():
        packed = None
        for group in range(GROUPS):
            block = total_ref[:, group * width : (group + 1) * width].astype(jnp.bfloat16)
            pick = unpack_rows(slots, sources, group)
            term = lax.dot_general(
                pick, block, (((0,), (0,)), ((), ())), preferred_element_type=jnp.float32
            )
            packed = term if packed is None else packed + term
        out_ref[...] = packed.astype(jnp.bfloat16)


def expert_apply(rows, weights, slots, sources, chunk=256):
    count, channels = rows.shape
    units = weights.shape[1]
    packed, width = count * GROUPS, channels // GROUPS
    return pl.pallas_call(
        functools.partial(expert_kernel, slots, sources),
        grid=(units // chunk,),
        in_specs=[
            pl.BlockSpec((count, channels), lambda i: (0, 0)),
            pl.BlockSpec((3, chunk, channels), lambda i: (0, i, 0)),
        ],
        out_specs=pl.BlockSpec((packed, width), lambda i: (0, 0)),
        out_shape=jax.ShapeDtypeStruct((packed, width), jnp.bfloat16),
        scratch_shapes=[pltpu.VMEM((count, channels), jnp.float32)],
        compiler_params=pltpu.CompilerParams(vmem_limit_bytes=48 * 1024 * 1024),
        cost_estimate=pl.CostEstimate(
            flops=6 * count * units * channels,
            bytes_accessed=6 * units * channels + 4 * packed * width,
            transcendentals=count * units,
        ),
    )(rows, weights)


def collect_kernel(row_ref, members_ref, *refs):
    pieces, state_ref, taps_ref, total_ref = refs[:-3], *refs[-3:]
    size_y, size_x = len(pieces), pieces[0].shape[0]
    lanes = state_ref.shape[1]
    total_ref[...] = jnp.zeros_like(total_ref)
    for step in range(size_y):
        source = lax.rem(row_ref[0] - step + size_y, size_y)
        for k in range(size_x):
            member = members_ref[source * size_x + k]
            total_ref[member] += pieces[step][k].astype(jnp.float32)
    state_ref[...] = total_ref[:, :lanes]
    taps_ref[...] = total_ref[:, lanes:]


def collect(row, members, pieces, prompts):
    size_x, rows, lanes = pieces[0].shape
    vmem, smem = pl.BlockSpec(memory_space=pltpu.VMEM), pl.BlockSpec(memory_space=pltpu.SMEM)
    return pl.pallas_call(
        collect_kernel,
        in_specs=[smem, smem] + [vmem] * len(pieces),
        out_specs=[vmem, vmem],
        out_shape=[
            jax.ShapeDtypeStruct((prompts, rows - 16, lanes), jnp.float32),
            jax.ShapeDtypeStruct((prompts, 16, lanes), jnp.float32),
        ],
        scratch_shapes=[pltpu.VMEM((prompts, rows, lanes), jnp.float32)],
        compiler_params=pltpu.CompilerParams(vmem_limit_bytes=16 * 1024 * 1024),
        cost_estimate=pl.CostEstimate(
            flops=len(pieces) * size_x * rows * lanes,
            bytes_accessed=2 * len(pieces) * size_x * rows * lanes,
            transcendentals=0,
        ),
    )(row, members, *pieces)


def neighbours(size_x, size_z):
    return [
        [x * size_z + z for x in (low, size_x - 1 - low) for z in range(size_z)]
        for low in range(size_x // 2)
    ]


def shards(
    ssm_input,
    b_inputs,
    c_readout,
    step_raw,
    decay_rate,
    skip_gain,
    conv_weight,
    prompt_state,
    prompt_taps,
    group_index,
    lengths,
    mixed_grad,
    expert_index,
    route_gain,
    gate_weight,
    up_weight,
    down_weight,
):
    steps_n, row_width = ssm_input.shape
    prompts, own_heads, head_size, state_n = prompt_state.shape
    taps_n, lanes = prompt_taps.shape[2] // head_size, own_heads * head_size
    owners = lax.axis_size(PLANE)
    lines, expert_count = lax.axis_size(("xh", "z")), lax.axis_size(("z", "c"))
    state_rows = own_heads * head_size

    stacked = jnp.concatenate([gate_weight, up_weight, down_weight], 0)
    size_x, size_z = lax.axis_size(("xh", "xl")), lax.axis_size("z")
    swap = []
    for x in range(size_x):
        half, other = x // (size_x // 2), size_x - 1 - x
        swap += [(x * 2 + half, x * 2 + half), (x * 2 + 1 - half, other * 2 + half)]
    swapped = lax.ppermute(stacked, ("xh", "xl", "c"), swap)
    weights = lax.all_gather(swapped, ("y", "xl", "c"), axis=1, tiled=True)

    row = lax.axis_index("y").astype(jnp.int32)[None]

    own_taps = jnp.transpose(
        prompt_taps.reshape(prompts, own_heads, taps_n, head_size), (0, 2, 1, 3)
    ).reshape(prompts * taps_n, lanes)
    own_member = jnp.broadcast_to(group_index.astype(jnp.bfloat16)[:, None], (1, lanes))
    notice = jnp.concatenate(
        [own_taps, own_member, jnp.zeros((7 - prompts * taps_n, lanes), jnp.bfloat16)], 0
    )
    notices = lax.all_to_all(
        jnp.broadcast_to(notice[None], (owners,) + notice.shape), PLANE, 0, 0, tiled=True
    )
    members = notices[:, prompts * taps_n, 0] > 0.5
    mine = group_index[0] == 1
    prior = jnp.where(mine, notices[:, taps_n : 2 * taps_n], notices[:, :taps_n])
    prior = jnp.transpose(prior, (1, 0, 2)).reshape(taps_n, row_width).astype(jnp.float32)
    prior = jnp.concatenate([jnp.zeros((8 - taps_n, row_width), jnp.float32), prior], 0)

    held = prompt_state.reshape(prompts, state_rows, state_n)
    outgoing_state = jnp.where(members[:, None, None], held[1][None], held[0][None])
    state = lax.all_to_all(outgoing_state, PLANE, 0, 0, tiled=True).reshape(row_width, state_n)

    step_size = jax.nn.softplus(step_raw)
    base, outgoing_grad, grow = mixer_base(
        lengths,
        row,
        ssm_input,
        prior,
        conv_weight,
        jnp.repeat(skip_gain, head_size)[None, :],
        mixed_grad,
        b_inputs,
        c_readout,
        step_size,
        decay_rate[None, :],
        head_size,
        (lax.axis_size("y"), lax.axis_size(("xh", "xl"))),
    )
    column_grad = lax.all_to_all(outgoing_grad, ("xh", "xl"), 0, 0, tiled=True)

    slots = 3 * steps_n // (2 * expert_count)
    width = row_width // GROUPS
    chosen = expert_index[:, 0]
    order = lax.iota(jnp.int32, steps_n)
    before = (chosen[:, None] == chosen[None, :]) & (order[:, None] < order[None, :])
    slot = jnp.sum(before.astype(jnp.int32), axis=0)
    place = (chosen % 2) * (lines // 2) + chosen // 2
    spot = (place * (GROUPS * slots) + slot)[None, :]
    packed_rows = lines * GROUPS * slots
    outgoing = dispatch(lengths, base, state, c_readout, grow, spot, head_size, slots, packed_rows)
    arrived = lax.all_to_all(
        outgoing.reshape(lines, GROUPS * slots, width),
        LINE,
        0,
        0,
        tiled=True,
        axis_index_groups=neighbours(size_x, size_z),
    )
    expert_rows = unpack(arrived.reshape(packed_rows, width), slots, lines)
    produced = expert_apply(expert_rows, weights, slots, lines)
    produced, column_grad = lax.optimization_barrier((produced, column_grad))
    returned = lax.all_to_all(
        produced.reshape(lines, GROUPS * slots, width),
        LINE,
        0,
        0,
        tiled=True,
        axis_index_groups=neighbours(size_x, size_z),
    ).reshape(packed_rows, width)
    spots = lax.iota(jnp.int32, packed_rows)
    placing = [
        (spots[:, None] == spot + group * slots).astype(jnp.bfloat16) for group in range(GROUPS)
    ]
    per_token = jnp.concatenate(
        [
            lax.dot_general(
                placing[group], returned, (((0,), (0,)), ((), ())), preferred_element_type=jnp.float32
            )
            for group in range(GROUPS)
        ],
        1,
    )
    size_y = lax.axis_size("y")
    pieces = [column_grad[:, 0]] + [
        lax.ppermute(column_grad[:, d], "y", [(i, (i + d) % size_y) for i in range(size_y)])
        for d in range(1, size_y)
    ]
    state_sum, taps_sum = collect(row, members.astype(jnp.int32), pieces, prompts)
    state_grad = state_sum.reshape(prompts, own_heads, head_size, state_n)
    taps_grad = jnp.transpose(
        taps_sum[:, :taps_n].reshape(prompts, taps_n, own_heads, head_size), (0, 2, 1, 3)
    ).reshape(prompts, own_heads, taps_n * head_size)
    moe_out = (route_gain * per_token).astype(jnp.bfloat16)
    return (moe_out, state_grad, taps_grad)


def solution(mesh):
    prompt, dp, expert = (mesh.shape[name] for name in ("prompt", "dp", "expert"))
    fine = Mesh(mesh.devices.reshape(prompt, 2, dp // 2, expert // 2, 2), AXES)
    tokens = P(AXES, None)
    single = P(AXES)
    experts, plane = ("z", "c"), PLANE
    return jax.shard_map(
        shards,
        mesh=fine,
        in_specs=(
            tokens,
            tokens,
            tokens,
            tokens,
            P(),
            P(),
            P(),
            P(experts, plane, None, None),
            P(experts, plane, None),
            single,
            single,
            tokens,
            tokens,
            tokens,
            P(experts, plane, None),
            P(experts, plane, None),
            P(experts, plane, None),
        ),
        out_specs=(
            tokens,
            P(experts, plane, None, None),
            P(experts, plane, None),
        ),
        check_vma=False,
    )
```

```python
import functools

import jax
import jax.numpy as jnp
from jax import lax
from jax.experimental import pallas as pl
from jax.experimental.pallas import tpu as pltpu
from jax.sharding import Mesh
from jax.sharding import PartitionSpec as P

AXES = ("y", "xh", "xl", "z", "c")
PLANE = ("y", "xh", "xl")
LINE = ("xh", "xl", "z")
GROUPS = 4


def spread(values, first, width, head_size):
    heads = values.shape[1]
    head = lax.broadcasted_iota(jnp.int32, (heads, width), 0)
    channel = lax.broadcasted_iota(jnp.int32, (heads, width), 1) + first
    pick = (channel // head_size == head).astype(jnp.float32)
    return jnp.dot(values, pick, precision=lax.Precision.HIGHEST, preferred_element_type=jnp.float32)


def mixer_kernel(
    head_size,
    length_ref,
    row_ref,
    x_ref,
    prior_ref,
    conv_ref,
    skip_ref,
    grad_ref,
    b_ref,
    c_ref,
    step_ref,
    rate_ref,
    base_ref,
    sent_ref,
    grow_ref,
    series_ref,
    scores_ref,
    first_ref,
    decay_ref,
):
    step = pl.program_id(0)
    steps_n, width = x_ref.shape
    exact = dict(precision=lax.Precision.HIGHEST, preferred_element_type=jnp.float32)
    across = (((1,), (1,)), ((), ()))
    down = (((0,), (0,)), ((), ()))

    @pl.when(step == 0)
    def _():
        row = lax.broadcasted_iota(jnp.int32, (steps_n, steps_n), 0)
        col = lax.broadcasted_iota(jnp.int32, (steps_n, steps_n), 1)
        scores = lax.dot_general(
            c_ref[...], b_ref[...], across, preferred_element_type=jnp.float32
        )
        scores_ref[...] = jnp.where(row >= col, scores, 0.0)
        turned = lax.dot_general(
            b_ref[...], c_ref[...], across, preferred_element_type=jnp.float32
        )
        first_ref[...] = jnp.where(col >= row, turned, 0.0)[: first_ref.shape[0]]
        lower = (row >= col).astype(jnp.float32)
        decay_sum = jnp.dot(lower, -step_ref[...] * rate_ref[...], **exact)
        grow_ref[...] = jnp.exp(decay_sum)
        decay_ref[...] = step_ref[...] * jnp.exp(-decay_sum)

    grow = spread(grow_ref[...], step * width, width, head_size)
    shrink = spread(decay_ref[...], step * width, width, head_size)
    series_ref[0:8] = prior_ref[...]
    series_ref[8 : 8 + steps_n] = x_ref[...].astype(jnp.float32)
    taps = [conv_ref[k : k + 1] for k in range(4)]
    summed = taps[3] * series_ref[8 : 8 + steps_n]
    for k in range(3):
        summed = summed + taps[k] * series_ref[5 + k : 5 + k + steps_n]
    conv_out = summed * jax.nn.sigmoid(summed)
    skip = skip_ref[...]
    inner = jnp.dot(scores_ref[...], conv_out * shrink, **exact)
    base_ref[...] = grow * inner + skip * conv_out

    live = lax.broadcasted_iota(jnp.int32, (steps_n, width), 0) < length_ref[0]
    given = jnp.where(live, grad_ref[...].astype(jnp.float32), 0.0)
    scaled = grow * given
    high = scaled.astype(jnp.bfloat16)
    low = (scaled - high.astype(jnp.float32)).astype(jnp.bfloat16)
    c_rows = c_ref[...]
    state_grad = (
        lax.dot_general(high, c_rows, down, preferred_element_type=jnp.float32)
        + lax.dot_general(low, c_rows, down, preferred_element_type=jnp.float32)
    ).astype(jnp.bfloat16)
    early = first_ref.shape[0]
    conv_grad = shrink[:early] * jnp.dot(first_ref[...], scaled, **exact) + skip * given[:early]
    gate = jax.nn.sigmoid(summed[:early])
    series_grad = conv_grad * gate * (1.0 + summed[:early] * (1.0 - gate))
    one, two, three = (series_grad[k : k + 1] for k in range(3))
    places = sent_ref.shape[0]
    lanes = width // places
    taps_rows = sent_ref.shape[2] - lanes
    taps_grad = jnp.concatenate(
        [
            taps[0] * one,
            taps[1] * one + taps[0] * two,
            taps[2] * one + taps[1] * two + taps[0] * three,
            jnp.zeros((taps_rows - 3, width), jnp.float32),
        ],
        0,
    ).astype(jnp.bfloat16)
    for k in range(places):
        sent_ref[k, 0, :lanes] = state_grad[k * lanes : (k + 1) * lanes]
        sent_ref[k, 0, lanes:] = taps_grad[:, k * lanes : (k + 1) * lanes]


def mixer_base(
    length, row, x_rows, prior, conv_weight, skip, grads, b_rows, c_rows, step_size, rate, head_size, owners
):
    steps_n, channels = x_rows.shape
    heads, state_n = step_size.shape[1], c_rows.shape[1]
    owners_y, owners_x = owners
    lanes = channels // (owners_y * owners_x)
    block = owners_x * lanes
    whole = lambda *shape: pl.BlockSpec(shape, lambda i, *_: (0,) * len(shape))
    part = lambda rows: pl.BlockSpec((rows, block), lambda i, *_: (0, i))
    sent = (owners_x, owners_y, lanes + 16, state_n)
    return pl.pallas_call(
        functools.partial(mixer_kernel, head_size),
        grid_spec=pltpu.PrefetchScalarGridSpec(
            num_scalar_prefetch=2,
            grid=(owners_y,),
            in_specs=[
                part(steps_n),
                part(8),
                part(4),
                part(1),
                part(steps_n),
                whole(steps_n, state_n),
                whole(steps_n, state_n),
                whole(steps_n, heads),
                whole(1, heads),
            ],
            out_specs=[
                part(steps_n),
                pl.BlockSpec(
                    (owners_x, 1, lanes + 16, state_n),
                    lambda i, _, row_ref: (0, lax.rem(i - row_ref[0] + owners_y, owners_y), 0, 0),
                ),
                whole(steps_n, heads),
            ],
            scratch_shapes=[
                pltpu.VMEM((8 + steps_n, block), jnp.float32),
                pltpu.VMEM((steps_n, steps_n), jnp.float32),
                pltpu.VMEM((8, steps_n), jnp.float32),
                pltpu.VMEM((steps_n, heads), jnp.float32),
            ],
        ),
        out_shape=[
            jax.ShapeDtypeStruct((steps_n, channels), jnp.float32),
            jax.ShapeDtypeStruct(sent, jnp.bfloat16),
            jax.ShapeDtypeStruct((steps_n, heads), jnp.float32),
        ],
        compiler_params=pltpu.CompilerParams(vmem_limit_bytes=32 * 1024 * 1024),
        cost_estimate=pl.CostEstimate(
            flops=20 * steps_n * channels * state_n,
            bytes_accessed=10 * steps_n * channels,
            transcendentals=steps_n * channels,
        ),
    )(length, row, x_rows, prior, conv_weight, skip, grads, b_rows, c_rows, step_size, rate)


def dispatch_kernel(
    head_size, slots, length_ref, base_ref, state_ref, c_ref, grow_ref, spot_ref, out_ref, total_ref
):
    group = pl.program_id(0)
    steps_n, width = base_ref.shape
    carried = lax.dot_general(
        c_ref[...], state_ref[...], (((1,), (1,)), ((), ())), preferred_element_type=jnp.float32
    )
    grow = spread(grow_ref[...], group * width, width, head_size)
    live = lax.broadcasted_iota(jnp.int32, (steps_n, width), 0) < length_ref[0]
    rows = jnp.where(live, base_ref[...] + grow * carried, 0.0).astype(jnp.bfloat16)
    packed = out_ref.shape[0]
    spots = lax.broadcasted_iota(jnp.int32, (packed, steps_n), 0)
    placing = (spots == spot_ref[...] + group * slots).astype(jnp.bfloat16)
    term = jnp.dot(placing, rows, preferred_element_type=jnp.float32)

    @pl.when(group == 0)
    def _():
        total_ref[...] = term

    @pl.when(group > 0)
    def _():
        total_ref[...] += term

    @pl.when(group == GROUPS - 1)
    def _():
        out_ref[...] = total_ref[...].astype(jnp.bfloat16)


def dispatch(length, base, state, c_rows, grow, spot, head_size, slots, packed):
    steps_n, channels = base.shape
    state_n, heads, width = state.shape[1], grow.shape[1], channels // GROUPS
    return pl.pallas_call(
        functools.partial(dispatch_kernel, head_size, slots),
        grid=(GROUPS,),
        in_specs=[
            pl.BlockSpec(memory_space=pltpu.SMEM),
            pl.BlockSpec((steps_n, width), lambda g: (0, g)),
            pl.BlockSpec((width, state_n), lambda g: (g, 0)),
            pl.BlockSpec((steps_n, state_n), lambda g: (0, 0)),
            pl.BlockSpec((steps_n, heads), lambda g: (0, 0)),
            pl.BlockSpec((1, steps_n), lambda g: (0, 0)),
        ],
        out_specs=pl.BlockSpec((packed, width), lambda g: (0, 0)),
        out_shape=jax.ShapeDtypeStruct((packed, width), jnp.bfloat16),
        scratch_shapes=[pltpu.VMEM((packed, width), jnp.float32)],
        compiler_params=pltpu.CompilerParams(vmem_limit_bytes=32 * 1024 * 1024),
        cost_estimate=pl.CostEstimate(
            flops=2 * channels * steps_n * (packed + state_n),
            bytes_accessed=6 * channels * steps_n + 2 * packed * width,
            transcendentals=0,
        ),
    )(length, base, state, c_rows, grow, spot)


def unpack_rows(slots, sources, group):
    count, total = sources * slots, sources * GROUPS * slots
    row = lax.broadcasted_iota(jnp.int32, (count, total), 0)
    col = lax.broadcasted_iota(jnp.int32, (count, total), 1)
    wanted = (row // slots) * (GROUPS * slots) + group * slots + row % slots
    return (col == wanted).astype(jnp.bfloat16)


def unpack_kernel(slots, sources, arrived_ref, rows_ref):
    pick = unpack_rows(slots, sources, pl.program_id(0))
    rows_ref[...] = jnp.dot(
        pick, arrived_ref[...], preferred_element_type=jnp.float32
    ).astype(jnp.bfloat16)


def unpack(arrived, slots, sources):
    packed, width = arrived.shape
    count = slots * sources
    return pl.pallas_call(
        functools.partial(unpack_kernel, slots, sources),
        grid=(GROUPS,),
        in_specs=[pl.BlockSpec((packed, width), lambda g: (0, 0))],
        out_specs=pl.BlockSpec((count, width), lambda g: (0, g)),
        out_shape=jax.ShapeDtypeStruct((count, GROUPS * width), jnp.bfloat16),
        compiler_params=pltpu.CompilerParams(vmem_limit_bytes=24 * 1024 * 1024),
        cost_estimate=pl.CostEstimate(
            flops=2 * GROUPS * count * packed * width,
            bytes_accessed=4 * packed * width,
            transcendentals=0,
        ),
    )(arrived)


def expert_kernel(slots, sources, rows_ref, weight_ref, out_ref, total_ref):
    step = pl.program_id(0)
    width = out_ref.shape[1]
    dims = (((1,), (1,)), ((), ()))
    rows = rows_ref[...]
    gate = lax.dot_general(rows, weight_ref[0], dims, preferred_element_type=jnp.float32)
    upper = lax.dot_general(rows, weight_ref[1], dims, preferred_element_type=jnp.float32)
    hidden = (jax.nn.silu(gate) * upper).astype(jnp.bfloat16)
    part = jnp.dot(hidden, weight_ref[2], preferred_element_type=jnp.float32)

    @pl.when(step == 0)
    def _():
        total_ref[...] = part

    @pl.when(step > 0)
    def _():
        total_ref[...] += part

    @pl.when(step == pl.num_programs(0) - 1)
    def _():
        packed = None
        for group in range(GROUPS):
            block = total_ref[:, group * width : (group + 1) * width].astype(jnp.bfloat16)
            pick = unpack_rows(slots, sources, group)
            term = lax.dot_general(
                pick, block, (((0,), (0,)), ((), ())), preferred_element_type=jnp.float32
            )
            packed = term if packed is None else packed + term
        out_ref[...] = packed.astype(jnp.bfloat16)


def expert_apply(rows, weights, slots, sources, chunk=256):
    count, channels = rows.shape
    units = weights.shape[1]
    packed, width = count * GROUPS, channels // GROUPS
    return pl.pallas_call(
        functools.partial(expert_kernel, slots, sources),
        grid=(units // chunk,),
        in_specs=[
            pl.BlockSpec((count, channels), lambda i: (0, 0)),
            pl.BlockSpec((3, chunk, channels), lambda i: (0, i, 0)),
        ],
        out_specs=pl.BlockSpec((packed, width), lambda i: (0, 0)),
        out_shape=jax.ShapeDtypeStruct((packed, width), jnp.bfloat16),
        scratch_shapes=[pltpu.VMEM((count, channels), jnp.float32)],
        compiler_params=pltpu.CompilerParams(vmem_limit_bytes=48 * 1024 * 1024),
        cost_estimate=pl.CostEstimate(
            flops=6 * count * units * channels,
            bytes_accessed=6 * units * channels + 4 * packed * width,
            transcendentals=count * units,
        ),
    )(rows, weights)


def presum_kernel(row_ref, members_ref, column_ref, out_ref, total_ref):
    size_x = column_ref.shape[0]
    total_ref[...] = jnp.zeros_like(total_ref)
    for k in range(size_x):
        member = members_ref[row_ref[0] * size_x + k]
        total_ref[member] += column_ref[k, 0].astype(jnp.float32)
    out_ref[0] = total_ref[...].astype(jnp.bfloat16)


def presum(row, members, column, prompts):
    size_x, size_y, rows, lanes = column.shape
    smem = pl.BlockSpec(memory_space=pltpu.SMEM)
    return pl.pallas_call(
        presum_kernel,
        grid=(size_y,),
        in_specs=[smem, smem, pl.BlockSpec((size_x, 1, rows, lanes), lambda i: (0, i, 0, 0))],
        out_specs=pl.BlockSpec((1, prompts, rows, lanes), lambda i: (i, 0, 0, 0)),
        out_shape=jax.ShapeDtypeStruct((size_y, prompts, rows, lanes), jnp.bfloat16),
        scratch_shapes=[pltpu.VMEM((prompts, rows, lanes), jnp.float32)],
        compiler_params=pltpu.CompilerParams(vmem_limit_bytes=16 * 1024 * 1024),
        cost_estimate=pl.CostEstimate(
            flops=size_x * size_y * rows * lanes,
            bytes_accessed=3 * size_x * size_y * rows * lanes,
            transcendentals=0,
        ),
    )(row, members, column)


def collect_kernel(*refs):
    pieces, (state_ref, taps_ref) = refs[:-2], refs[-2:]
    lanes = state_ref.shape[1]
    total = pieces[0][...].astype(jnp.float32)
    for piece in pieces[1:]:
        total = total + piece[...].astype(jnp.float32)
    state_ref[...] = total[:, :lanes]
    taps_ref[...] = total[:, lanes:]


def collect(pieces):
    prompts, rows, lanes = pieces[0].shape
    vmem = pl.BlockSpec(memory_space=pltpu.VMEM)
    return pl.pallas_call(
        collect_kernel,
        in_specs=[vmem] * len(pieces),
        out_specs=[vmem, vmem],
        out_shape=[
            jax.ShapeDtypeStruct((prompts, rows - 16, lanes), jnp.float32),
            jax.ShapeDtypeStruct((prompts, 16, lanes), jnp.float32),
        ],
        compiler_params=pltpu.CompilerParams(vmem_limit_bytes=16 * 1024 * 1024),
        cost_estimate=pl.CostEstimate(
            flops=len(pieces) * prompts * rows * lanes,
            bytes_accessed=2 * len(pieces) * prompts * rows * lanes,
            transcendentals=0,
        ),
    )(*pieces)


def neighbours(size_x, size_z):
    return [
        [x * size_z + z for x in (low, size_x - 1 - low) for z in range(size_z)]
        for low in range(size_x // 2)
    ]


def shards(
    ssm_input,
    b_inputs,
    c_readout,
    step_raw,
    decay_rate,
    skip_gain,
    conv_weight,
    prompt_state,
    prompt_taps,
    group_index,
    lengths,
    mixed_grad,
    expert_index,
    route_gain,
    gate_weight,
    up_weight,
    down_weight,
):
    steps_n, row_width = ssm_input.shape
    prompts, own_heads, head_size, state_n = prompt_state.shape
    taps_n, lanes = prompt_taps.shape[2] // head_size, own_heads * head_size
    owners = lax.axis_size(PLANE)
    lines, expert_count = lax.axis_size(("xh", "z")), lax.axis_size(("z", "c"))
    state_rows = own_heads * head_size

    stacked = jnp.concatenate([gate_weight, up_weight, down_weight], 0)
    size_x, size_z = lax.axis_size(("xh", "xl")), lax.axis_size("z")
    swap = []
    for x in range(size_x):
        half, other = x // (size_x // 2), size_x - 1 - x
        swap += [(x * 2 + half, x * 2 + half), (x * 2 + 1 - half, other * 2 + half)]
    swapped = lax.ppermute(stacked, ("xh", "xl", "c"), swap)
    weights = lax.all_gather(swapped, ("y", "xl", "c"), axis=1, tiled=True)

    row = lax.axis_index("y").astype(jnp.int32)[None]

    own_taps = jnp.transpose(
        prompt_taps.reshape(prompts, own_heads, taps_n, head_size), (0, 2, 1, 3)
    ).reshape(prompts * taps_n, lanes)
    own_member = jnp.broadcast_to(group_index.astype(jnp.bfloat16)[:, None], (1, lanes))
    notice = jnp.concatenate(
        [own_taps, own_member, jnp.zeros((7 - prompts * taps_n, lanes), jnp.bfloat16)], 0
    )
    notices = lax.all_to_all(
        jnp.broadcast_to(notice[None], (owners,) + notice.shape), PLANE, 0, 0, tiled=True
    )
    members = notices[:, prompts * taps_n, 0] > 0.5
    mine = group_index[0] == 1
    prior = jnp.where(mine, notices[:, taps_n : 2 * taps_n], notices[:, :taps_n])
    prior = jnp.transpose(prior, (1, 0, 2)).reshape(taps_n, row_width).astype(jnp.float32)
    prior = jnp.concatenate([jnp.zeros((8 - taps_n, row_width), jnp.float32), prior], 0)

    held = prompt_state.reshape(prompts, state_rows, state_n)
    outgoing_state = jnp.where(members[:, None, None], held[1][None], held[0][None])
    state = lax.all_to_all(outgoing_state, PLANE, 0, 0, tiled=True).reshape(row_width, state_n)

    step_size = jax.nn.softplus(step_raw)
    base, outgoing_grad, grow = mixer_base(
        lengths,
        row,
        ssm_input,
        prior,
        conv_weight,
        jnp.repeat(skip_gain, head_size)[None, :],
        mixed_grad,
        b_inputs,
        c_readout,
        step_size,
        decay_rate[None, :],
        head_size,
        (lax.axis_size("y"), lax.axis_size(("xh", "xl"))),
    )

    slots = 3 * steps_n // (2 * expert_count)
    width = row_width // GROUPS
    chosen = expert_index[:, 0]
    order = lax.iota(jnp.int32, steps_n)
    before = (chosen[:, None] == chosen[None, :]) & (order[:, None] < order[None, :])
    slot = jnp.sum(before.astype(jnp.int32), axis=0)
    place = (chosen % 2) * (lines // 2) + chosen // 2
    spot = (place * (GROUPS * slots) + slot)[None, :]
    packed_rows = lines * GROUPS * slots
    outgoing = dispatch(lengths, base, state, c_readout, grow, spot, head_size, slots, packed_rows)
    arrived = lax.all_to_all(
        outgoing.reshape(lines, GROUPS * slots, width),
        LINE,
        0,
        0,
        tiled=True,
        axis_index_groups=neighbours(size_x, size_z),
    )
    arrived, outgoing_grad = lax.optimization_barrier((arrived, outgoing_grad))
    column_grad = lax.all_to_all(outgoing_grad, ("xh", "xl"), 0, 0, tiled=True)
    expert_rows = unpack(arrived.reshape(packed_rows, width), slots, lines)
    produced = expert_apply(expert_rows, weights, slots, lines)
    row_grad = presum(row, members.astype(jnp.int32), column_grad, prompts)
    produced, row_grad = lax.optimization_barrier((produced, row_grad))
    returned = lax.all_to_all(
        produced.reshape(lines, GROUPS * slots, width),
        LINE,
        0,
        0,
        tiled=True,
        axis_index_groups=neighbours(size_x, size_z),
    ).reshape(packed_rows, width)
    spots = lax.iota(jnp.int32, packed_rows)
    placing = [
        (spots[:, None] == spot + group * slots).astype(jnp.bfloat16) for group in range(GROUPS)
    ]
    per_token = jnp.concatenate(
        [
            lax.dot_general(
                placing[group], returned, (((0,), (0,)), ((), ())), preferred_element_type=jnp.float32
            )
            for group in range(GROUPS)
        ],
        1,
    )
    size_y = lax.axis_size("y")
    pieces = [row_grad[0]] + [
        lax.ppermute(row_grad[d], "y", [(i, (i + d) % size_y) for i in range(size_y)])
        for d in range(1, size_y)
    ]
    state_sum, taps_sum = collect(pieces)
    state_grad = state_sum.reshape(prompts, own_heads, head_size, state_n)
    taps_grad = jnp.transpose(
        taps_sum[:, :taps_n].reshape(prompts, taps_n, own_heads, head_size), (0, 2, 1, 3)
    ).reshape(prompts, own_heads, taps_n * head_size)
    moe_out = (route_gain * per_token).astype(jnp.bfloat16)
    return (moe_out, state_grad, taps_grad)


def solution(mesh):
    prompt, dp, expert = (mesh.shape[name] for name in ("prompt", "dp", "expert"))
    fine = Mesh(mesh.devices.reshape(prompt, 2, dp // 2, expert // 2, 2), AXES)
    tokens = P(AXES, None)
    single = P(AXES)
    experts, plane = ("z", "c"), PLANE
    return jax.shard_map(
        shards,
        mesh=fine,
        in_specs=(
            tokens,
            tokens,
            tokens,
            tokens,
            P(),
            P(),
            P(),
            P(experts, plane, None, None),
            P(experts, plane, None),
            single,
            single,
            tokens,
            tokens,
            tokens,
            P(experts, plane, None),
            P(experts, plane, None),
            P(experts, plane, None),
        ),
        out_specs=(
            tokens,
            P(experts, plane, None, None),
            P(experts, plane, None),
        ),
        check_vma=False,
    )
```

```python
import functools

import jax
import jax.numpy as jnp
from jax import lax
from jax.experimental import pallas as pl
from jax.experimental.pallas import tpu as pltpu
from jax.sharding import Mesh
from jax.sharding import PartitionSpec as P

AXES = ("y", "xh", "xl", "z", "c")
PLANE = ("y", "xh", "xl")
LINE = ("xh", "xl", "z")
GROUPS = 4


def spread(values, first, width, head_size):
    heads = values.shape[1]
    head = lax.broadcasted_iota(jnp.int32, (heads, width), 0)
    channel = lax.broadcasted_iota(jnp.int32, (heads, width), 1) + first
    pick = (channel // head_size == head).astype(jnp.float32)
    return jnp.dot(values, pick, precision=lax.Precision.HIGHEST, preferred_element_type=jnp.float32)


def mixer_kernel(
    head_size,
    length_ref,
    row_ref,
    x_ref,
    prior_ref,
    conv_ref,
    skip_ref,
    grad_ref,
    b_ref,
    c_ref,
    step_ref,
    rate_ref,
    base_ref,
    sent_ref,
    grow_ref,
    series_ref,
    scores_ref,
    first_ref,
    decay_ref,
):
    step = pl.program_id(0)
    steps_n, width = x_ref.shape
    exact = dict(precision=lax.Precision.HIGHEST, preferred_element_type=jnp.float32)
    across = (((1,), (1,)), ((), ()))
    down = (((0,), (0,)), ((), ()))

    @pl.when(step == 0)
    def _():
        row = lax.broadcasted_iota(jnp.int32, (steps_n, steps_n), 0)
        col = lax.broadcasted_iota(jnp.int32, (steps_n, steps_n), 1)
        scores = lax.dot_general(
            c_ref[...], b_ref[...], across, preferred_element_type=jnp.float32
        )
        scores_ref[...] = jnp.where(row >= col, scores, 0.0)
        turned = lax.dot_general(
            b_ref[...], c_ref[...], across, preferred_element_type=jnp.float32
        )
        first_ref[...] = jnp.where(col >= row, turned, 0.0)[: first_ref.shape[0]]
        lower = (row >= col).astype(jnp.float32)
        decay_sum = jnp.dot(lower, -step_ref[...] * rate_ref[...], **exact)
        grow_ref[...] = jnp.exp(decay_sum)
        decay_ref[...] = step_ref[...] * jnp.exp(-decay_sum)

    grow = spread(grow_ref[...], step * width, width, head_size)
    shrink = spread(decay_ref[...], step * width, width, head_size)
    series_ref[0:8] = prior_ref[...]
    series_ref[8 : 8 + steps_n] = x_ref[...].astype(jnp.float32)
    taps = [conv_ref[k : k + 1] for k in range(4)]
    summed = taps[3] * series_ref[8 : 8 + steps_n]
    for k in range(3):
        summed = summed + taps[k] * series_ref[5 + k : 5 + k + steps_n]
    conv_out = summed * jax.nn.sigmoid(summed)
    skip = skip_ref[...]
    inner = jnp.dot(scores_ref[...], conv_out * shrink, **exact)
    base_ref[...] = grow * inner + skip * conv_out

    live = lax.broadcasted_iota(jnp.int32, (steps_n, width), 0) < length_ref[0]
    given = jnp.where(live, grad_ref[...].astype(jnp.float32), 0.0)
    scaled = grow * given
    high = scaled.astype(jnp.bfloat16)
    low = (scaled - high.astype(jnp.float32)).astype(jnp.bfloat16)
    c_rows = c_ref[...]
    state_grad = (
        lax.dot_general(high, c_rows, down, preferred_element_type=jnp.float32)
        + lax.dot_general(low, c_rows, down, preferred_element_type=jnp.float32)
    ).astype(jnp.bfloat16)
    early = first_ref.shape[0]
    conv_grad = shrink[:early] * jnp.dot(first_ref[...], scaled, **exact) + skip * given[:early]
    gate = jax.nn.sigmoid(summed[:early])
    series_grad = conv_grad * gate * (1.0 + summed[:early] * (1.0 - gate))
    one, two, three = (series_grad[k : k + 1] for k in range(3))
    places = sent_ref.shape[0]
    lanes = width // places
    taps_rows = sent_ref.shape[2] - lanes
    taps_grad = jnp.concatenate(
        [
            taps[0] * one,
            taps[1] * one + taps[0] * two,
            taps[2] * one + taps[1] * two + taps[0] * three,
            jnp.zeros((taps_rows - 3, width), jnp.float32),
        ],
        0,
    ).astype(jnp.bfloat16)
    for k in range(places):
        slot = lax.rem(k - row_ref[1] + places, places)
        sent_ref[slot, 0, :lanes] = state_grad[k * lanes : (k + 1) * lanes]
        sent_ref[slot, 0, lanes:] = taps_grad[:, k * lanes : (k + 1) * lanes]


def mixer_base(
    length, row, x_rows, prior, conv_weight, skip, grads, b_rows, c_rows, step_size, rate, head_size, owners
):
    steps_n, channels = x_rows.shape
    heads, state_n = step_size.shape[1], c_rows.shape[1]
    owners_y, owners_x = owners
    lanes = channels // (owners_y * owners_x)
    block = owners_x * lanes
    whole = lambda *shape: pl.BlockSpec(shape, lambda i, *_: (0,) * len(shape))
    part = lambda rows: pl.BlockSpec((rows, block), lambda i, *_: (0, i))
    sent = (owners_x, owners_y, lanes + 16, state_n)
    return pl.pallas_call(
        functools.partial(mixer_kernel, head_size),
        grid_spec=pltpu.PrefetchScalarGridSpec(
            num_scalar_prefetch=2,
            grid=(owners_y,),
            in_specs=[
                part(steps_n),
                part(8),
                part(4),
                part(1),
                part(steps_n),
                whole(steps_n, state_n),
                whole(steps_n, state_n),
                whole(steps_n, heads),
                whole(1, heads),
            ],
            out_specs=[
                part(steps_n),
                pl.BlockSpec(
                    (owners_x, 1, lanes + 16, state_n),
                    lambda i, _, row_ref: (0, lax.rem(i - row_ref[0] + owners_y, owners_y), 0, 0),
                ),
                whole(steps_n, heads),
            ],
            scratch_shapes=[
                pltpu.VMEM((8 + steps_n, block), jnp.float32),
                pltpu.VMEM((steps_n, steps_n), jnp.float32),
                pltpu.VMEM((8, steps_n), jnp.float32),
                pltpu.VMEM((steps_n, heads), jnp.float32),
            ],
        ),
        out_shape=[
            jax.ShapeDtypeStruct((steps_n, channels), jnp.float32),
            jax.ShapeDtypeStruct(sent, jnp.bfloat16),
            jax.ShapeDtypeStruct((steps_n, heads), jnp.float32),
        ],
        compiler_params=pltpu.CompilerParams(vmem_limit_bytes=32 * 1024 * 1024),
        cost_estimate=pl.CostEstimate(
            flops=20 * steps_n * channels * state_n,
            bytes_accessed=10 * steps_n * channels,
            transcendentals=steps_n * channels,
        ),
    )(length, row, x_rows, prior, conv_weight, skip, grads, b_rows, c_rows, step_size, rate)


def dispatch_kernel(
    head_size, slots, length_ref, base_ref, state_ref, c_ref, grow_ref, spot_ref, out_ref, total_ref
):
    group = pl.program_id(0)
    steps_n, width = base_ref.shape
    size_x, size_y = state_ref.shape[:2]
    lanes = width // (size_x * size_y)
    state = jnp.concatenate(
        [state_ref[x, y, :lanes] for y in range(size_y) for x in range(size_x)], 0
    )
    carried = lax.dot_general(
        c_ref[...], state, (((1,), (1,)), ((), ())), preferred_element_type=jnp.float32
    )
    grow = spread(grow_ref[...], group * width, width, head_size)
    live = lax.broadcasted_iota(jnp.int32, (steps_n, width), 0) < length_ref[0]
    rows = jnp.where(live, base_ref[...] + grow * carried, 0.0).astype(jnp.bfloat16)
    packed = out_ref.shape[0]
    spots = lax.broadcasted_iota(jnp.int32, (packed, steps_n), 0)
    placing = (spots == spot_ref[...] + group * slots).astype(jnp.bfloat16)
    term = jnp.dot(placing, rows, preferred_element_type=jnp.float32)

    @pl.when(group == 0)
    def _():
        total_ref[...] = term

    @pl.when(group > 0)
    def _():
        total_ref[...] += term

    @pl.when(group == GROUPS - 1)
    def _():
        out_ref[...] = total_ref[...].astype(jnp.bfloat16)


def dispatch(length, base, state, c_rows, grow, spot, head_size, slots, packed):
    steps_n, channels = base.shape
    size_x, size_y, state_rows, state_n = state.shape
    heads, width = grow.shape[1], channels // GROUPS
    return pl.pallas_call(
        functools.partial(dispatch_kernel, head_size, slots),
        grid=(GROUPS,),
        in_specs=[
            pl.BlockSpec(memory_space=pltpu.SMEM),
            pl.BlockSpec((steps_n, width), lambda g: (0, g)),
            pl.BlockSpec((size_x, size_y // GROUPS, state_rows, state_n), lambda g: (0, g, 0, 0)),
            pl.BlockSpec((steps_n, state_n), lambda g: (0, 0)),
            pl.BlockSpec((steps_n, heads), lambda g: (0, 0)),
            pl.BlockSpec((1, steps_n), lambda g: (0, 0)),
        ],
        out_specs=pl.BlockSpec((packed, width), lambda g: (0, 0)),
        out_shape=jax.ShapeDtypeStruct((packed, width), jnp.bfloat16),
        scratch_shapes=[pltpu.VMEM((packed, width), jnp.float32)],
        compiler_params=pltpu.CompilerParams(vmem_limit_bytes=32 * 1024 * 1024),
        cost_estimate=pl.CostEstimate(
            flops=2 * channels * steps_n * (packed + state_n),
            bytes_accessed=6 * channels * steps_n + 2 * packed * width,
            transcendentals=0,
        ),
    )(length, base, state, c_rows, grow, spot)


def unpack_rows(slots, sources, group):
    count, total = sources * slots, sources * GROUPS * slots
    row = lax.broadcasted_iota(jnp.int32, (count, total), 0)
    col = lax.broadcasted_iota(jnp.int32, (count, total), 1)
    wanted = (row // slots) * (GROUPS * slots) + group * slots + row % slots
    return (col == wanted).astype(jnp.bfloat16)


def unpack_kernel(slots, sources, arrived_ref, rows_ref):
    pick = unpack_rows(slots, sources, pl.program_id(0))
    rows_ref[...] = jnp.dot(
        pick, arrived_ref[...], preferred_element_type=jnp.float32
    ).astype(jnp.bfloat16)


def unpack(arrived, slots, sources):
    packed, width = arrived.shape
    count = slots * sources
    return pl.pallas_call(
        functools.partial(unpack_kernel, slots, sources),
        grid=(GROUPS,),
        in_specs=[pl.BlockSpec((packed, width), lambda g: (0, 0))],
        out_specs=pl.BlockSpec((count, width), lambda g: (0, g)),
        out_shape=jax.ShapeDtypeStruct((count, GROUPS * width), jnp.bfloat16),
        compiler_params=pltpu.CompilerParams(vmem_limit_bytes=24 * 1024 * 1024),
        cost_estimate=pl.CostEstimate(
            flops=2 * GROUPS * count * packed * width,
            bytes_accessed=4 * packed * width,
            transcendentals=0,
        ),
    )(arrived)


def expert_kernel(slots, sources, rows_ref, weight_ref, out_ref, total_ref):
    step = pl.program_id(0)
    width = out_ref.shape[1]
    dims = (((1,), (1,)), ((), ()))
    rows = rows_ref[...]
    gate = lax.dot_general(rows, weight_ref[0], dims, preferred_element_type=jnp.float32)
    upper = lax.dot_general(rows, weight_ref[1], dims, preferred_element_type=jnp.float32)
    hidden = (jax.nn.silu(gate) * upper).astype(jnp.bfloat16)
    part = jnp.dot(hidden, weight_ref[2], preferred_element_type=jnp.float32)

    @pl.when(step == 0)
    def _():
        total_ref[...] = part

    @pl.when(step > 0)
    def _():
        total_ref[...] += part

    @pl.when(step == pl.num_programs(0) - 1)
    def _():
        packed = None
        for group in range(GROUPS):
            block = total_ref[:, group * width : (group + 1) * width].astype(jnp.bfloat16)
            pick = unpack_rows(slots, sources, group)
            term = lax.dot_general(
                pick, block, (((0,), (0,)), ((), ())), preferred_element_type=jnp.float32
            )
            packed = term if packed is None else packed + term
        out_ref[...] = packed.astype(jnp.bfloat16)


def expert_apply(rows, weights, slots, sources, chunk=256):
    count, channels = rows.shape
    units = weights.shape[1]
    packed, width = count * GROUPS, channels // GROUPS
    return pl.pallas_call(
        functools.partial(expert_kernel, slots, sources),
        grid=(units // chunk,),
        in_specs=[
            pl.BlockSpec((count, channels), lambda i: (0, 0)),
            pl.BlockSpec((3, chunk, channels), lambda i: (0, i, 0)),
        ],
        out_specs=pl.BlockSpec((packed, width), lambda i: (0, 0)),
        out_shape=jax.ShapeDtypeStruct((packed, width), jnp.bfloat16),
        scratch_shapes=[pltpu.VMEM((count, channels), jnp.float32)],
        compiler_params=pltpu.CompilerParams(vmem_limit_bytes=48 * 1024 * 1024),
        cost_estimate=pl.CostEstimate(
            flops=6 * count * units * channels,
            bytes_accessed=6 * units * channels + 4 * packed * width,
            transcendentals=count * units,
        ),
    )(rows, weights)


def combine_kernel(slots, spot_ref, gain_ref, returned_ref, out_ref):
    steps_n, packed = out_ref.shape[0], returned_ref.shape[0]
    spots = lax.broadcasted_iota(jnp.int32, (steps_n, packed), 1)
    pick = (spots == spot_ref[...] + pl.program_id(0) * slots).astype(jnp.bfloat16)
    rows = jnp.dot(pick, returned_ref[...], preferred_element_type=jnp.float32)
    out_ref[...] = (gain_ref[...] * rows).astype(jnp.bfloat16)


def combine(spot, gain, returned, slots):
    packed, width = returned.shape
    steps_n = spot.shape[0]
    column = pl.BlockSpec((steps_n, 1), lambda g: (0, 0))
    return pl.pallas_call(
        functools.partial(combine_kernel, slots),
        grid=(GROUPS,),
        in_specs=[column, column, pl.BlockSpec((packed, width), lambda g: (0, 0))],
        out_specs=pl.BlockSpec((steps_n, width), lambda g: (0, g)),
        out_shape=jax.ShapeDtypeStruct((steps_n, GROUPS * width), jnp.bfloat16),
        compiler_params=pltpu.CompilerParams(vmem_limit_bytes=24 * 1024 * 1024),
        cost_estimate=pl.CostEstimate(
            flops=2 * GROUPS * steps_n * packed * width,
            bytes_accessed=2 * packed * width + 2 * GROUPS * steps_n * width,
            transcendentals=0,
        ),
    )(spot, gain, returned)


def presum_kernel(members_ref, *refs):
    pieces, (out_ref, total_ref) = refs[:-2], refs[-2:]
    total_ref[...] = jnp.zeros_like(total_ref)
    for k, piece in enumerate(pieces):
        total_ref[members_ref[k]] += piece[0].astype(jnp.float32)
    out_ref[0] = total_ref[...].astype(jnp.bfloat16)


def presum(members, pieces, prompts):
    size_y, rows, lanes = pieces[0].shape
    smem = pl.BlockSpec(memory_space=pltpu.SMEM)
    return pl.pallas_call(
        presum_kernel,
        grid=(size_y,),
        in_specs=[smem] + [pl.BlockSpec((1, rows, lanes), lambda i: (i, 0, 0))] * len(pieces),
        out_specs=pl.BlockSpec((1, prompts, rows, lanes), lambda i: (i, 0, 0, 0)),
        out_shape=jax.ShapeDtypeStruct((size_y, prompts, rows, lanes), jnp.bfloat16),
        scratch_shapes=[pltpu.VMEM((prompts, rows, lanes), jnp.float32)],
        compiler_params=pltpu.CompilerParams(vmem_limit_bytes=16 * 1024 * 1024),
        cost_estimate=pl.CostEstimate(
            flops=len(pieces) * size_y * rows * lanes,
            bytes_accessed=3 * len(pieces) * size_y * rows * lanes,
            transcendentals=0,
        ),
    )(members, *pieces)


def collect_kernel(*refs):
    pieces, (state_ref, taps_ref) = refs[:-2], refs[-2:]
    lanes = state_ref.shape[1]
    total = pieces[0][...].astype(jnp.float32)
    for piece in pieces[1:]:
        total = total + piece[...].astype(jnp.float32)
    state_ref[...] = total[:, :lanes]
    taps_ref[...] = total[:, lanes:]


def collect(pieces):
    prompts, rows, lanes = pieces[0].shape
    vmem = pl.BlockSpec(memory_space=pltpu.VMEM)
    return pl.pallas_call(
        collect_kernel,
        in_specs=[vmem] * len(pieces),
        out_specs=[vmem, vmem],
        out_shape=[
            jax.ShapeDtypeStruct((prompts, rows - 16, lanes), jnp.float32),
            jax.ShapeDtypeStruct((prompts, 16, lanes), jnp.float32),
        ],
        compiler_params=pltpu.CompilerParams(vmem_limit_bytes=16 * 1024 * 1024),
        cost_estimate=pl.CostEstimate(
            flops=len(pieces) * prompts * rows * lanes,
            bytes_accessed=2 * len(pieces) * prompts * rows * lanes,
            transcendentals=0,
        ),
    )(*pieces)


def neighbours(size_x, size_z):
    return [
        [x * size_z + z for x in (low, size_x - 1 - low) for z in range(size_z)]
        for low in range(size_x // 2)
    ]


def shards(
    ssm_input,
    b_inputs,
    c_readout,
    step_raw,
    decay_rate,
    skip_gain,
    conv_weight,
    prompt_state,
    prompt_taps,
    group_index,
    lengths,
    mixed_grad,
    expert_index,
    route_gain,
    gate_weight,
    up_weight,
    down_weight,
):
    steps_n, row_width = ssm_input.shape
    prompts, own_heads, head_size, state_n = prompt_state.shape
    taps_n, lanes = prompt_taps.shape[2] // head_size, own_heads * head_size
    lines, expert_count = lax.axis_size(("xh", "z")), lax.axis_size(("z", "c"))
    state_rows = own_heads * head_size

    stacked = jnp.concatenate([gate_weight, up_weight, down_weight], 0)
    size_x, size_z = lax.axis_size(("xh", "xl")), lax.axis_size("z")
    swap = []
    for x in range(size_x):
        half, other = x // (size_x // 2), size_x - 1 - x
        swap += [(x * 2 + half, x * 2 + half), (x * 2 + 1 - half, other * 2 + half)]
    swapped = lax.ppermute(stacked, ("xh", "xl", "c"), swap)
    weights = lax.all_gather(swapped, ("y", "xl", "c"), axis=1, tiled=True)

    size_y = lax.axis_size("y")
    x_axes = ("xh", "xl")
    x_index = lax.axis_index(x_axes).astype(jnp.int32)
    place_here = jnp.stack([lax.axis_index("y").astype(jnp.int32), x_index])

    own_taps = jnp.transpose(
        prompt_taps.reshape(prompts, own_heads, taps_n, head_size), (0, 2, 1, 3)
    ).reshape(prompts, taps_n, lanes)
    held = jnp.concatenate(
        [
            prompt_state.reshape(prompts, state_rows, state_n),
            own_taps,
            jnp.zeros((prompts, 16 - taps_n, lanes), jnp.bfloat16),
        ],
        1,
    )
    column_state = lax.all_to_all(
        jnp.broadcast_to(held[None], (size_y,) + held.shape), "y", 0, 0, tiled=True
    )
    back = [group_index] + [
        lax.ppermute(group_index, x_axes, [(i, (i + d) % size_x) for i in range(size_x)])
        for d in range(1, size_x)
    ]
    behind = jnp.concatenate(back)
    steps_back = (x_index - lax.iota(jnp.int32, size_x)) % size_x
    picked = steps_back[:, None] == lax.iota(jnp.int32, size_x)[None, :]
    row_members = jnp.sum(jnp.where(picked, behind[None, :], 0), axis=1)
    state = lax.all_to_all(
        jnp.where(
            (row_members == 1)[:, None, None, None], column_state[:, 1][None], column_state[:, 0][None]
        ),
        x_axes,
        0,
        0,
        tiled=True,
    )
    prior = jnp.transpose(state[:, :, state_rows : state_rows + taps_n], (2, 1, 0, 3))
    prior = prior.reshape(taps_n, row_width).astype(jnp.float32)
    prior = jnp.concatenate([jnp.zeros((8 - taps_n, row_width), jnp.float32), prior], 0)

    step_size = jax.nn.softplus(step_raw)
    base, outgoing_grad, grow = mixer_base(
        lengths,
        place_here,
        ssm_input,
        prior,
        conv_weight,
        jnp.repeat(skip_gain, head_size)[None, :],
        mixed_grad,
        b_inputs,
        c_readout,
        step_size,
        decay_rate[None, :],
        head_size,
        (size_y, size_x),
    )

    slots = 3 * steps_n // (2 * expert_count)
    width = row_width // GROUPS
    chosen = expert_index[:, 0]
    order = lax.iota(jnp.int32, steps_n)
    before = (chosen[:, None] == chosen[None, :]) & (order[:, None] < order[None, :])
    slot = jnp.sum(before.astype(jnp.int32), axis=0)
    place = (chosen % 2) * (lines // 2) + chosen // 2
    spot = (place * (GROUPS * slots) + slot)[None, :]
    packed_rows = lines * GROUPS * slots
    outgoing = dispatch(lengths, base, state, c_readout, grow, spot, head_size, slots, packed_rows)
    arrived = lax.all_to_all(
        outgoing.reshape(lines, GROUPS * slots, width),
        LINE,
        0,
        0,
        tiled=True,
        axis_index_groups=neighbours(size_x, size_z),
    )
    expert_rows = unpack(arrived.reshape(packed_rows, width), slots, lines)
    weights, *leaving = lax.optimization_barrier(
        (weights, *(outgoing_grad[d] for d in range(size_x)))
    )
    column_grad = [leaving[0]] + [
        lax.ppermute(leaving[d], x_axes, [(i, (i + d) % size_x) for i in range(size_x)])
        for d in range(1, size_x)
    ]
    produced = expert_apply(expert_rows, weights, slots, lines)
    row_grad = presum(behind, column_grad, prompts)
    returned = lax.all_to_all(
        produced.reshape(lines, GROUPS * slots, width),
        LINE,
        0,
        0,
        tiled=True,
        axis_index_groups=neighbours(size_x, size_z),
    ).reshape(packed_rows, width)
    pieces = [row_grad[0]] + [
        lax.ppermute(row_grad[d], "y", [(i, (i + d) % size_y) for i in range(size_y)])
        for d in range(1, size_y)
    ]
    state_sum, taps_sum = collect(pieces)
    state_grad = state_sum.reshape(prompts, own_heads, head_size, state_n)
    taps_grad = jnp.transpose(
        taps_sum[:, :taps_n].reshape(prompts, taps_n, own_heads, head_size), (0, 2, 1, 3)
    ).reshape(prompts, own_heads, taps_n * head_size)
    moe_out = combine(jnp.transpose(spot), route_gain, returned, slots)
    return (moe_out, state_grad, taps_grad)


def solution(mesh):
    prompt, dp, expert = (mesh.shape[name] for name in ("prompt", "dp", "expert"))
    fine = Mesh(mesh.devices.reshape(prompt, 2, dp // 2, expert // 2, 2), AXES)
    tokens = P(AXES, None)
    single = P(AXES)
    experts, plane = ("z", "c"), PLANE
    return jax.shard_map(
        shards,
        mesh=fine,
        in_specs=(
            tokens,
            tokens,
            tokens,
            tokens,
            P(),
            P(),
            P(),
            P(experts, plane, None, None),
            P(experts, plane, None),
            single,
            single,
            tokens,
            tokens,
            tokens,
            P(experts, plane, None),
            P(experts, plane, None),
            P(experts, plane, None),
        ),
        out_specs=(
            tokens,
            P(experts, plane, None, None),
            P(experts, plane, None),
        ),
        check_vma=False,
    )
```

```python
import functools

import jax
import jax.numpy as jnp
from jax import lax
from jax.experimental import pallas as pl
from jax.experimental.pallas import tpu as pltpu
from jax.sharding import Mesh
from jax.sharding import PartitionSpec as P

AXES = ("y", "xh", "xl", "z", "c")
PLANE = ("y", "xh", "xl")
LINE = ("xh", "xl", "z")
GROUPS = 4


def spread(values, first, width, head_size):
    heads = values.shape[1]
    head = lax.broadcasted_iota(jnp.int32, (heads, width), 0)
    channel = lax.broadcasted_iota(jnp.int32, (heads, width), 1) + first
    pick = (channel // head_size == head).astype(jnp.float32)
    return jnp.dot(values, pick, precision=lax.Precision.HIGHEST, preferred_element_type=jnp.float32)


def mixer_kernel(
    head_size,
    length_ref,
    row_ref,
    x_ref,
    prior_ref,
    conv_ref,
    skip_ref,
    grad_ref,
    b_ref,
    c_ref,
    step_ref,
    rate_ref,
    base_ref,
    sent_ref,
    grow_ref,
    series_ref,
    scores_ref,
    first_ref,
    decay_ref,
):
    step = pl.program_id(0)
    steps_n, width = x_ref.shape
    exact = dict(precision=lax.Precision.HIGHEST, preferred_element_type=jnp.float32)
    across = (((1,), (1,)), ((), ()))
    down = (((0,), (0,)), ((), ()))

    @pl.when(step == 0)
    def _():
        row = lax.broadcasted_iota(jnp.int32, (steps_n, steps_n), 0)
        col = lax.broadcasted_iota(jnp.int32, (steps_n, steps_n), 1)
        scores = lax.dot_general(
            c_ref[...], b_ref[...], across, preferred_element_type=jnp.float32
        )
        scores_ref[...] = jnp.where(row >= col, scores, 0.0)
        turned = lax.dot_general(
            b_ref[...], c_ref[...], across, preferred_element_type=jnp.float32
        )
        first_ref[...] = jnp.where(col >= row, turned, 0.0)[: first_ref.shape[0]]
        lower = (row >= col).astype(jnp.float32)
        decay_sum = jnp.dot(lower, -step_ref[...] * rate_ref[...], **exact)
        grow_ref[...] = jnp.exp(decay_sum)
        decay_ref[...] = step_ref[...] * jnp.exp(-decay_sum)

    grow = spread(grow_ref[...], step * width, width, head_size)
    shrink = spread(decay_ref[...], step * width, width, head_size)
    series_ref[0:8] = prior_ref[...]
    series_ref[8 : 8 + steps_n] = x_ref[...].astype(jnp.float32)
    taps = [conv_ref[k : k + 1] for k in range(4)]
    summed = taps[3] * series_ref[8 : 8 + steps_n]
    for k in range(3):
        summed = summed + taps[k] * series_ref[5 + k : 5 + k + steps_n]
    conv_out = summed * jax.nn.sigmoid(summed)
    skip = skip_ref[...]
    inner = jnp.dot(scores_ref[...], conv_out * shrink, **exact)
    base_ref[...] = grow * inner + skip * conv_out

    live = lax.broadcasted_iota(jnp.int32, (steps_n, width), 0) < length_ref[0]
    given = jnp.where(live, grad_ref[...].astype(jnp.float32), 0.0)
    scaled = grow * given
    high = scaled.astype(jnp.bfloat16)
    low = (scaled - high.astype(jnp.float32)).astype(jnp.bfloat16)
    c_rows = c_ref[...]
    state_grad = (
        lax.dot_general(high, c_rows, down, preferred_element_type=jnp.float32)
        + lax.dot_general(low, c_rows, down, preferred_element_type=jnp.float32)
    ).astype(jnp.bfloat16)
    early = first_ref.shape[0]
    conv_grad = shrink[:early] * jnp.dot(first_ref[...], scaled, **exact) + skip * given[:early]
    gate = jax.nn.sigmoid(summed[:early])
    series_grad = conv_grad * gate * (1.0 + summed[:early] * (1.0 - gate))
    one, two, three = (series_grad[k : k + 1] for k in range(3))
    places = sent_ref.shape[0]
    lanes = width // places
    taps_rows = sent_ref.shape[2] - lanes
    taps_grad = jnp.concatenate(
        [
            taps[0] * one,
            taps[1] * one + taps[0] * two,
            taps[2] * one + taps[1] * two + taps[0] * three,
            jnp.zeros((taps_rows - 3, width), jnp.float32),
        ],
        0,
    ).astype(jnp.bfloat16)
    for k in range(places):
        sent_ref[k, 0, :lanes] = state_grad[k * lanes : (k + 1) * lanes]
        sent_ref[k, 0, lanes:] = taps_grad[:, k * lanes : (k + 1) * lanes]


def mixer_base(
    length, row, x_rows, prior, conv_weight, skip, grads, b_rows, c_rows, step_size, rate, head_size, owners
):
    steps_n, channels = x_rows.shape
    heads, state_n = step_size.shape[1], c_rows.shape[1]
    owners_y, owners_x = owners
    lanes = channels // (owners_y * owners_x)
    block = owners_x * lanes
    whole = lambda *shape: pl.BlockSpec(shape, lambda i, *_: (0,) * len(shape))
    part = lambda rows: pl.BlockSpec((rows, block), lambda i, *_: (0, i))
    sent = (owners_x, owners_y, lanes + 16, state_n)
    return pl.pallas_call(
        functools.partial(mixer_kernel, head_size),
        grid_spec=pltpu.PrefetchScalarGridSpec(
            num_scalar_prefetch=2,
            grid=(owners_y,),
            in_specs=[
                part(steps_n),
                part(8),
                part(4),
                part(1),
                part(steps_n),
                whole(steps_n, state_n),
                whole(steps_n, state_n),
                whole(steps_n, heads),
                whole(1, heads),
            ],
            out_specs=[
                part(steps_n),
                pl.BlockSpec(
                    (owners_x, 1, lanes + 16, state_n),
                    lambda i, _, row_ref: (0, lax.rem(i - row_ref[0] + owners_y, owners_y), 0, 0),
                ),
                whole(steps_n, heads),
            ],
            scratch_shapes=[
                pltpu.VMEM((8 + steps_n, block), jnp.float32),
                pltpu.VMEM((steps_n, steps_n), jnp.float32),
                pltpu.VMEM((8, steps_n), jnp.float32),
                pltpu.VMEM((steps_n, heads), jnp.float32),
            ],
        ),
        out_shape=[
            jax.ShapeDtypeStruct((steps_n, channels), jnp.float32),
            jax.ShapeDtypeStruct(sent, jnp.bfloat16),
            jax.ShapeDtypeStruct((steps_n, heads), jnp.float32),
        ],
        compiler_params=pltpu.CompilerParams(vmem_limit_bytes=32 * 1024 * 1024),
        cost_estimate=pl.CostEstimate(
            flops=20 * steps_n * channels * state_n,
            bytes_accessed=10 * steps_n * channels,
            transcendentals=steps_n * channels,
        ),
    )(length, row, x_rows, prior, conv_weight, skip, grads, b_rows, c_rows, step_size, rate)


def dispatch_kernel(
    head_size, slots, length_ref, base_ref, state_ref, c_ref, grow_ref, spot_ref, out_ref, total_ref
):
    group = pl.program_id(0)
    steps_n, width = base_ref.shape
    size_x, size_y = state_ref.shape[:2]
    lanes = width // (size_x * size_y)
    state = jnp.concatenate(
        [state_ref[x, y, :lanes] for y in range(size_y) for x in range(size_x)], 0
    )
    carried = lax.dot_general(
        c_ref[...], state, (((1,), (1,)), ((), ())), preferred_element_type=jnp.float32
    )
    grow = spread(grow_ref[...], group * width, width, head_size)
    live = lax.broadcasted_iota(jnp.int32, (steps_n, width), 0) < length_ref[0]
    rows = jnp.where(live, base_ref[...] + grow * carried, 0.0).astype(jnp.bfloat16)
    packed = out_ref.shape[0]
    spots = lax.broadcasted_iota(jnp.int32, (packed, steps_n), 0)
    placing = (spots == spot_ref[...] + group * slots).astype(jnp.bfloat16)
    term = jnp.dot(placing, rows, preferred_element_type=jnp.float32)

    @pl.when(group == 0)
    def _():
        total_ref[...] = term

    @pl.when(group > 0)
    def _():
        total_ref[...] += term

    @pl.when(group == GROUPS - 1)
    def _():
        out_ref[...] = total_ref[...].astype(jnp.bfloat16)


def dispatch(length, base, state, c_rows, grow, spot, head_size, slots, packed):
    steps_n, channels = base.shape
    size_x, size_y, state_rows, state_n = state.shape
    heads, width = grow.shape[1], channels // GROUPS
    return pl.pallas_call(
        functools.partial(dispatch_kernel, head_size, slots),
        grid=(GROUPS,),
        in_specs=[
            pl.BlockSpec(memory_space=pltpu.SMEM),
            pl.BlockSpec((steps_n, width), lambda g: (0, g)),
            pl.BlockSpec((size_x, size_y // GROUPS, state_rows, state_n), lambda g: (0, g, 0, 0)),
            pl.BlockSpec((steps_n, state_n), lambda g: (0, 0)),
            pl.BlockSpec((steps_n, heads), lambda g: (0, 0)),
            pl.BlockSpec((1, steps_n), lambda g: (0, 0)),
        ],
        out_specs=pl.BlockSpec((packed, width), lambda g: (0, 0)),
        out_shape=jax.ShapeDtypeStruct((packed, width), jnp.bfloat16),
        scratch_shapes=[pltpu.VMEM((packed, width), jnp.float32)],
        compiler_params=pltpu.CompilerParams(vmem_limit_bytes=32 * 1024 * 1024),
        cost_estimate=pl.CostEstimate(
            flops=2 * channels * steps_n * (packed + state_n),
            bytes_accessed=6 * channels * steps_n + 2 * packed * width,
            transcendentals=0,
        ),
    )(length, base, state, c_rows, grow, spot)


def unpack_rows(slots, sources, group):
    count, total = sources * slots, sources * GROUPS * slots
    row = lax.broadcasted_iota(jnp.int32, (count, total), 0)
    col = lax.broadcasted_iota(jnp.int32, (count, total), 1)
    wanted = (row // slots) * (GROUPS * slots) + group * slots + row % slots
    return (col == wanted).astype(jnp.bfloat16)


def unpack_kernel(slots, sources, arrived_ref, rows_ref):
    pick = unpack_rows(slots, sources, pl.program_id(0))
    rows_ref[...] = jnp.dot(
        pick, arrived_ref[...], preferred_element_type=jnp.float32
    ).astype(jnp.bfloat16)


def unpack(arrived, slots, sources):
    packed, width = arrived.shape
    count = slots * sources
    return pl.pallas_call(
        functools.partial(unpack_kernel, slots, sources),
        grid=(GROUPS,),
        in_specs=[pl.BlockSpec((packed, width), lambda g: (0, 0))],
        out_specs=pl.BlockSpec((count, width), lambda g: (0, g)),
        out_shape=jax.ShapeDtypeStruct((count, GROUPS * width), jnp.bfloat16),
        compiler_params=pltpu.CompilerParams(vmem_limit_bytes=24 * 1024 * 1024),
        cost_estimate=pl.CostEstimate(
            flops=2 * GROUPS * count * packed * width,
            bytes_accessed=4 * packed * width,
            transcendentals=0,
        ),
    )(arrived)


def expert_kernel(slots, sources, rows_ref, weight_ref, out_ref, total_ref):
    step = pl.program_id(0)
    width = out_ref.shape[1]
    dims = (((1,), (1,)), ((), ()))
    rows = rows_ref[...]
    gate = lax.dot_general(rows, weight_ref[0], dims, preferred_element_type=jnp.float32)
    upper = lax.dot_general(rows, weight_ref[1], dims, preferred_element_type=jnp.float32)
    hidden = (jax.nn.silu(gate) * upper).astype(jnp.bfloat16)
    part = jnp.dot(hidden, weight_ref[2], preferred_element_type=jnp.float32)

    @pl.when(step == 0)
    def _():
        total_ref[...] = part

    @pl.when(step > 0)
    def _():
        total_ref[...] += part

    @pl.when(step == pl.num_programs(0) - 1)
    def _():
        packed = None
        for group in range(GROUPS):
            block = total_ref[:, group * width : (group + 1) * width].astype(jnp.bfloat16)
            pick = unpack_rows(slots, sources, group)
            term = lax.dot_general(
                pick, block, (((0,), (0,)), ((), ())), preferred_element_type=jnp.float32
            )
            packed = term if packed is None else packed + term
        out_ref[...] = packed.astype(jnp.bfloat16)


def expert_apply(rows, weights, slots, sources, chunk=256):
    count, channels = rows.shape
    units = weights.shape[1]
    packed, width = count * GROUPS, channels // GROUPS
    return pl.pallas_call(
        functools.partial(expert_kernel, slots, sources),
        grid=(units // chunk,),
        in_specs=[
            pl.BlockSpec((count, channels), lambda i: (0, 0)),
            pl.BlockSpec((3, chunk, channels), lambda i: (0, i, 0)),
        ],
        out_specs=pl.BlockSpec((packed, width), lambda i: (0, 0)),
        out_shape=jax.ShapeDtypeStruct((packed, width), jnp.bfloat16),
        scratch_shapes=[pltpu.VMEM((count, channels), jnp.float32)],
        compiler_params=pltpu.CompilerParams(vmem_limit_bytes=48 * 1024 * 1024),
        cost_estimate=pl.CostEstimate(
            flops=6 * count * units * channels,
            bytes_accessed=6 * units * channels + 4 * packed * width,
            transcendentals=count * units,
        ),
    )(rows, weights)


def combine_kernel(slots, spot_ref, gain_ref, returned_ref, out_ref):
    steps_n, packed = out_ref.shape[0], returned_ref.shape[0]
    spots = lax.broadcasted_iota(jnp.int32, (steps_n, packed), 1)
    pick = (spots == spot_ref[...] + pl.program_id(0) * slots).astype(jnp.bfloat16)
    rows = jnp.dot(pick, returned_ref[...], preferred_element_type=jnp.float32)
    out_ref[...] = (gain_ref[...] * rows).astype(jnp.bfloat16)


def combine(spot, gain, returned, slots):
    packed, width = returned.shape
    steps_n = spot.shape[0]
    column = pl.BlockSpec((steps_n, 1), lambda g: (0, 0))
    return pl.pallas_call(
        functools.partial(combine_kernel, slots),
        grid=(GROUPS,),
        in_specs=[column, column, pl.BlockSpec((packed, width), lambda g: (0, 0))],
        out_specs=pl.BlockSpec((steps_n, width), lambda g: (0, g)),
        out_shape=jax.ShapeDtypeStruct((steps_n, GROUPS * width), jnp.bfloat16),
        compiler_params=pltpu.CompilerParams(vmem_limit_bytes=24 * 1024 * 1024),
        cost_estimate=pl.CostEstimate(
            flops=2 * GROUPS * steps_n * packed * width,
            bytes_accessed=2 * packed * width + 2 * GROUPS * steps_n * width,
            transcendentals=0,
        ),
    )(spot, gain, returned)


def presum_kernel(members_ref, column_ref, out_ref, total_ref):
    total_ref[...] = jnp.zeros_like(total_ref)
    for k in range(column_ref.shape[0]):
        total_ref[members_ref[k]] += column_ref[k, 0].astype(jnp.float32)
    out_ref[0] = total_ref[...].astype(jnp.bfloat16)


def presum(members, column, prompts):
    size_x, size_y, rows, lanes = column.shape
    smem = pl.BlockSpec(memory_space=pltpu.SMEM)
    return pl.pallas_call(
        presum_kernel,
        grid=(size_y,),
        in_specs=[smem, pl.BlockSpec((size_x, 1, rows, lanes), lambda i: (0, i, 0, 0))],
        out_specs=pl.BlockSpec((1, prompts, rows, lanes), lambda i: (i, 0, 0, 0)),
        out_shape=jax.ShapeDtypeStruct((size_y, prompts, rows, lanes), jnp.bfloat16),
        scratch_shapes=[pltpu.VMEM((prompts, rows, lanes), jnp.float32)],
        compiler_params=pltpu.CompilerParams(vmem_limit_bytes=16 * 1024 * 1024),
        cost_estimate=pl.CostEstimate(
            flops=size_x * size_y * rows * lanes,
            bytes_accessed=3 * size_x * size_y * rows * lanes,
            transcendentals=0,
        ),
    )(members, column)


def collect_kernel(*refs):
    pieces, (state_ref, taps_ref) = refs[:-2], refs[-2:]
    lanes = state_ref.shape[1]
    total = pieces[0][...].astype(jnp.float32)
    for piece in pieces[1:]:
        total = total + piece[...].astype(jnp.float32)
    state_ref[...] = total[:, :lanes]
    taps_ref[...] = total[:, lanes:]


def collect(pieces):
    prompts, rows, lanes = pieces[0].shape
    vmem = pl.BlockSpec(memory_space=pltpu.VMEM)
    return pl.pallas_call(
        collect_kernel,
        in_specs=[vmem] * len(pieces),
        out_specs=[vmem, vmem],
        out_shape=[
            jax.ShapeDtypeStruct((prompts, rows - 16, lanes), jnp.float32),
            jax.ShapeDtypeStruct((prompts, 16, lanes), jnp.float32),
        ],
        compiler_params=pltpu.CompilerParams(vmem_limit_bytes=16 * 1024 * 1024),
        cost_estimate=pl.CostEstimate(
            flops=len(pieces) * prompts * rows * lanes,
            bytes_accessed=2 * len(pieces) * prompts * rows * lanes,
            transcendentals=0,
        ),
    )(*pieces)


def neighbours(size_x, size_z):
    return [
        [x * size_z + z for x in (low, size_x - 1 - low) for z in range(size_z)]
        for low in range(size_x // 2)
    ]


def shards(
    ssm_input,
    b_inputs,
    c_readout,
    step_raw,
    decay_rate,
    skip_gain,
    conv_weight,
    prompt_state,
    prompt_taps,
    group_index,
    lengths,
    mixed_grad,
    expert_index,
    route_gain,
    gate_weight,
    up_weight,
    down_weight,
):
    steps_n, row_width = ssm_input.shape
    prompts, own_heads, head_size, state_n = prompt_state.shape
    taps_n, lanes = prompt_taps.shape[2] // head_size, own_heads * head_size
    lines, expert_count = lax.axis_size(("xh", "z")), lax.axis_size(("z", "c"))
    state_rows = own_heads * head_size

    stacked = jnp.concatenate([gate_weight, up_weight, down_weight], 0)
    size_x, size_z = lax.axis_size(("xh", "xl")), lax.axis_size("z")
    swap = []
    for x in range(size_x):
        half, other = x // (size_x // 2), size_x - 1 - x
        swap += [(x * 2 + half, x * 2 + half), (x * 2 + 1 - half, other * 2 + half)]
    swapped = lax.ppermute(stacked, ("xh", "xl", "c"), swap)
    weights = lax.all_gather(swapped, ("y", "xl", "c"), axis=1, tiled=True)

    size_y = lax.axis_size("y")
    x_axes = ("xh", "xl")
    x_index = lax.axis_index(x_axes).astype(jnp.int32)
    row = lax.axis_index("y").astype(jnp.int32)[None]

    own_taps = jnp.transpose(
        prompt_taps.reshape(prompts, own_heads, taps_n, head_size), (0, 2, 1, 3)
    ).reshape(prompts, taps_n, lanes)
    held = jnp.concatenate(
        [
            prompt_state.reshape(prompts, state_rows, state_n),
            own_taps,
            jnp.zeros((prompts, 16 - taps_n, lanes), jnp.bfloat16),
        ],
        1,
    )
    column_state = lax.all_to_all(
        jnp.broadcast_to(held[None], (size_y,) + held.shape), "y", 0, 0, tiled=True
    )
    back = [group_index] + [
        lax.ppermute(group_index, x_axes, [(i, (i + d) % size_x) for i in range(size_x)])
        for d in range(1, size_x)
    ]
    behind = jnp.concatenate(back)
    steps_back = (x_index - lax.iota(jnp.int32, size_x)) % size_x
    picked = steps_back[:, None] == lax.iota(jnp.int32, size_x)[None, :]
    row_members = jnp.sum(jnp.where(picked, behind[None, :], 0), axis=1)
    state = lax.all_to_all(
        jnp.where(
            (row_members == 1)[:, None, None, None], column_state[:, 1][None], column_state[:, 0][None]
        ),
        x_axes,
        0,
        0,
        tiled=True,
    )
    prior = jnp.transpose(state[:, :, state_rows : state_rows + taps_n], (2, 1, 0, 3))
    prior = prior.reshape(taps_n, row_width).astype(jnp.float32)
    prior = jnp.concatenate([jnp.zeros((8 - taps_n, row_width), jnp.float32), prior], 0)

    step_size = jax.nn.softplus(step_raw)
    base, outgoing_grad, grow = mixer_base(
        lengths,
        row,
        ssm_input,
        prior,
        conv_weight,
        jnp.repeat(skip_gain, head_size)[None, :],
        mixed_grad,
        b_inputs,
        c_readout,
        step_size,
        decay_rate[None, :],
        head_size,
        (size_y, size_x),
    )

    slots = 3 * steps_n // (2 * expert_count)
    width = row_width // GROUPS
    chosen = expert_index[:, 0]
    order = lax.iota(jnp.int32, steps_n)
    before = (chosen[:, None] == chosen[None, :]) & (order[:, None] < order[None, :])
    slot = jnp.sum(before.astype(jnp.int32), axis=0)
    place = (chosen % 2) * (lines // 2) + chosen // 2
    spot = (place * (GROUPS * slots) + slot)[None, :]
    packed_rows = lines * GROUPS * slots
    outgoing = dispatch(lengths, base, state, c_readout, grow, spot, head_size, slots, packed_rows)
    arrived = lax.all_to_all(
        outgoing.reshape(lines, GROUPS * slots, width),
        LINE,
        0,
        0,
        tiled=True,
        axis_index_groups=neighbours(size_x, size_z),
    )
    arrived, outgoing_grad = lax.optimization_barrier((arrived, outgoing_grad))
    column_grad = lax.all_to_all(outgoing_grad, x_axes, 0, 0, tiled=True)
    expert_rows = unpack(arrived.reshape(packed_rows, width), slots, lines)
    produced = expert_apply(expert_rows, weights, slots, lines)
    produced, column_grad = lax.optimization_barrier((produced, column_grad))
    row_grad = presum(row_members, column_grad, prompts)
    returned = lax.all_to_all(
        produced.reshape(lines, GROUPS * slots, width),
        LINE,
        0,
        0,
        tiled=True,
        axis_index_groups=neighbours(size_x, size_z),
    ).reshape(packed_rows, width)
    pieces = [row_grad[0]] + [
        lax.ppermute(row_grad[d], "y", [(i, (i + d) % size_y) for i in range(size_y)])
        for d in range(1, size_y)
    ]
    state_sum, taps_sum = collect(pieces)
    state_grad = state_sum.reshape(prompts, own_heads, head_size, state_n)
    taps_grad = jnp.transpose(
        taps_sum[:, :taps_n].reshape(prompts, taps_n, own_heads, head_size), (0, 2, 1, 3)
    ).reshape(prompts, own_heads, taps_n * head_size)
    moe_out = combine(jnp.transpose(spot), route_gain, returned, slots)
    return (moe_out, state_grad, taps_grad)


def solution(mesh):
    prompt, dp, expert = (mesh.shape[name] for name in ("prompt", "dp", "expert"))
    fine = Mesh(mesh.devices.reshape(prompt, 2, dp // 2, expert // 2, 2), AXES)
    tokens = P(AXES, None)
    single = P(AXES)
    experts, plane = ("z", "c"), PLANE
    return jax.shard_map(
        shards,
        mesh=fine,
        in_specs=(
            tokens,
            tokens,
            tokens,
            tokens,
            P(),
            P(),
            P(),
            P(experts, plane, None, None),
            P(experts, plane, None),
            single,
            single,
            tokens,
            tokens,
            tokens,
            P(experts, plane, None),
            P(experts, plane, None),
            P(experts, plane, None),
        ),
        out_specs=(
            tokens,
            P(experts, plane, None, None),
            P(experts, plane, None),
        ),
        check_vma=False,
    )
```

```python
import functools

import jax
import jax.numpy as jnp
from jax import lax
from jax.experimental import pallas as pl
from jax.experimental.pallas import tpu as pltpu
from jax.sharding import Mesh
from jax.sharding import PartitionSpec as P

AXES = ("y", "xh", "xl", "z", "c")
PLANE = ("y", "xh", "xl")
LINE = ("xh", "xl", "z")
GROUPS = 4


def spread(values, first, width, head_size):
    heads = values.shape[1]
    head = lax.broadcasted_iota(jnp.int32, (heads, width), 0)
    channel = lax.broadcasted_iota(jnp.int32, (heads, width), 1) + first
    pick = (channel // head_size == head).astype(jnp.float32)
    return jnp.dot(values, pick, precision=lax.Precision.HIGHEST, preferred_element_type=jnp.float32)


def mixer_kernel(
    head_size,
    length_ref,
    row_ref,
    x_ref,
    prior_ref,
    conv_ref,
    skip_ref,
    grad_ref,
    b_ref,
    c_ref,
    step_ref,
    rate_ref,
    base_ref,
    sent_ref,
    grow_ref,
    series_ref,
    scores_ref,
    first_ref,
    decay_ref,
):
    step = pl.program_id(0)
    steps_n, width = x_ref.shape
    exact = dict(precision=lax.Precision.HIGHEST, preferred_element_type=jnp.float32)
    across = (((1,), (1,)), ((), ()))
    down = (((0,), (0,)), ((), ()))

    @pl.when(step == 0)
    def _():
        row = lax.broadcasted_iota(jnp.int32, (steps_n, steps_n), 0)
        col = lax.broadcasted_iota(jnp.int32, (steps_n, steps_n), 1)
        scores = lax.dot_general(
            c_ref[...], b_ref[...], across, preferred_element_type=jnp.float32
        )
        scores_ref[...] = jnp.where(row >= col, scores, 0.0)
        turned = lax.dot_general(
            b_ref[...], c_ref[...], across, preferred_element_type=jnp.float32
        )
        first_ref[...] = jnp.where(col >= row, turned, 0.0)[: first_ref.shape[0]]
        lower = (row >= col).astype(jnp.float32)
        decay_sum = jnp.dot(lower, -step_ref[...] * rate_ref[...], **exact)
        grow_ref[...] = jnp.exp(decay_sum)
        decay_ref[...] = step_ref[...] * jnp.exp(-decay_sum)

    grow = spread(grow_ref[...], step * width, width, head_size)
    shrink = spread(decay_ref[...], step * width, width, head_size)
    series_ref[0:8] = prior_ref[...]
    series_ref[8 : 8 + steps_n] = x_ref[...].astype(jnp.float32)
    taps = [conv_ref[k : k + 1] for k in range(4)]
    summed = taps[3] * series_ref[8 : 8 + steps_n]
    for k in range(3):
        summed = summed + taps[k] * series_ref[5 + k : 5 + k + steps_n]
    conv_out = summed * jax.nn.sigmoid(summed)
    skip = skip_ref[...]
    inner = jnp.dot(scores_ref[...], conv_out * shrink, **exact)
    base_ref[...] = grow * inner + skip * conv_out

    live = lax.broadcasted_iota(jnp.int32, (steps_n, width), 0) < length_ref[0]
    given = jnp.where(live, grad_ref[...].astype(jnp.float32), 0.0)
    scaled = grow * given
    high = scaled.astype(jnp.bfloat16)
    low = (scaled - high.astype(jnp.float32)).astype(jnp.bfloat16)
    c_rows = c_ref[...]
    state_grad = (
        lax.dot_general(high, c_rows, down, preferred_element_type=jnp.float32)
        + lax.dot_general(low, c_rows, down, preferred_element_type=jnp.float32)
    ).astype(jnp.bfloat16)
    early = first_ref.shape[0]
    conv_grad = shrink[:early] * jnp.dot(first_ref[...], scaled, **exact) + skip * given[:early]
    gate = jax.nn.sigmoid(summed[:early])
    series_grad = conv_grad * gate * (1.0 + summed[:early] * (1.0 - gate))
    one, two, three = (series_grad[k : k + 1] for k in range(3))
    places = sent_ref.shape[0]
    lanes = width // places
    taps_rows = sent_ref.shape[2] - lanes
    taps_grad = jnp.concatenate(
        [
            taps[0] * one,
            taps[1] * one + taps[0] * two,
            taps[2] * one + taps[1] * two + taps[0] * three,
            jnp.zeros((taps_rows - 3, width), jnp.float32),
        ],
        0,
    ).astype(jnp.bfloat16)
    for k in range(places):
        sent_ref[k, 0, :lanes] = state_grad[k * lanes : (k + 1) * lanes]
        sent_ref[k, 0, lanes:] = taps_grad[:, k * lanes : (k + 1) * lanes]


def mixer_base(
    length, row, x_rows, prior, conv_weight, skip, grads, b_rows, c_rows, step_size, rate, head_size, owners
):
    steps_n, channels = x_rows.shape
    heads, state_n = step_size.shape[1], c_rows.shape[1]
    owners_y, owners_x = owners
    lanes = channels // (owners_y * owners_x)
    block = owners_x * lanes
    whole = lambda *shape: pl.BlockSpec(shape, lambda i, *_: (0,) * len(shape))
    part = lambda rows: pl.BlockSpec((rows, block), lambda i, *_: (0, i))
    sent = (owners_x, owners_y, lanes + 16, state_n)
    return pl.pallas_call(
        functools.partial(mixer_kernel, head_size),
        grid_spec=pltpu.PrefetchScalarGridSpec(
            num_scalar_prefetch=2,
            grid=(owners_y,),
            in_specs=[
                part(steps_n),
                part(8),
                part(4),
                part(1),
                part(steps_n),
                whole(steps_n, state_n),
                whole(steps_n, state_n),
                whole(steps_n, heads),
                whole(1, heads),
            ],
            out_specs=[
                part(steps_n),
                pl.BlockSpec(
                    (owners_x, 1, lanes + 16, state_n),
                    lambda i, _, row_ref: (0, lax.rem(i - row_ref[0] + owners_y, owners_y), 0, 0),
                ),
                whole(steps_n, heads),
            ],
            scratch_shapes=[
                pltpu.VMEM((8 + steps_n, block), jnp.float32),
                pltpu.VMEM((steps_n, steps_n), jnp.float32),
                pltpu.VMEM((8, steps_n), jnp.float32),
                pltpu.VMEM((steps_n, heads), jnp.float32),
            ],
        ),
        out_shape=[
            jax.ShapeDtypeStruct((steps_n, channels), jnp.float32),
            jax.ShapeDtypeStruct(sent, jnp.bfloat16),
            jax.ShapeDtypeStruct((steps_n, heads), jnp.float32),
        ],
        compiler_params=pltpu.CompilerParams(vmem_limit_bytes=58 * 1024 * 1024),
        cost_estimate=pl.CostEstimate(
            flops=20 * steps_n * channels * state_n,
            bytes_accessed=10 * steps_n * channels,
            transcendentals=steps_n * channels,
        ),
    )(length, row, x_rows, prior, conv_weight, skip, grads, b_rows, c_rows, step_size, rate)


def dispatch_kernel(
    head_size, slots, length_ref, base_ref, state_ref, c_ref, grow_ref, spot_ref, out_ref, total_ref
):
    group = pl.program_id(0)
    steps_n, width = base_ref.shape
    size_x, size_y = state_ref.shape[:2]
    lanes = width // (size_x * size_y)
    state = jnp.concatenate(
        [state_ref[x, y, :lanes] for y in range(size_y) for x in range(size_x)], 0
    )
    carried = lax.dot_general(
        c_ref[...], state, (((1,), (1,)), ((), ())), preferred_element_type=jnp.float32
    )
    grow = spread(grow_ref[...], group * width, width, head_size)
    live = lax.broadcasted_iota(jnp.int32, (steps_n, width), 0) < length_ref[0]
    rows = jnp.where(live, base_ref[...] + grow * carried, 0.0).astype(jnp.bfloat16)
    packed = out_ref.shape[0]
    spots = lax.broadcasted_iota(jnp.int32, (packed, steps_n), 0)
    placing = (spots == spot_ref[...] + group * slots).astype(jnp.bfloat16)
    term = jnp.dot(placing, rows, preferred_element_type=jnp.float32)

    @pl.when(group == 0)
    def _():
        total_ref[...] = term

    @pl.when(group > 0)
    def _():
        total_ref[...] += term

    @pl.when(group == GROUPS - 1)
    def _():
        out_ref[...] = total_ref[...].astype(jnp.bfloat16)


def dispatch(length, base, state, c_rows, grow, spot, head_size, slots, packed):
    steps_n, channels = base.shape
    size_x, size_y, state_rows, state_n = state.shape
    heads, width = grow.shape[1], channels // GROUPS
    return pl.pallas_call(
        functools.partial(dispatch_kernel, head_size, slots),
        grid=(GROUPS,),
        in_specs=[
            pl.BlockSpec(memory_space=pltpu.SMEM),
            pl.BlockSpec((steps_n, width), lambda g: (0, g)),
            pl.BlockSpec((size_x, size_y // GROUPS, state_rows, state_n), lambda g: (0, g, 0, 0)),
            pl.BlockSpec((steps_n, state_n), lambda g: (0, 0)),
            pl.BlockSpec((steps_n, heads), lambda g: (0, 0)),
            pl.BlockSpec((1, steps_n), lambda g: (0, 0)),
        ],
        out_specs=pl.BlockSpec((packed, width), lambda g: (0, 0)),
        out_shape=jax.ShapeDtypeStruct((packed, width), jnp.bfloat16),
        scratch_shapes=[pltpu.VMEM((packed, width), jnp.float32)],
        compiler_params=pltpu.CompilerParams(vmem_limit_bytes=32 * 1024 * 1024),
        cost_estimate=pl.CostEstimate(
            flops=2 * channels * steps_n * (packed + state_n),
            bytes_accessed=6 * channels * steps_n + 2 * packed * width,
            transcendentals=0,
        ),
    )(length, base, state, c_rows, grow, spot)


def unpack_rows(slots, sources, group):
    count, total = sources * slots, sources * GROUPS * slots
    row = lax.broadcasted_iota(jnp.int32, (count, total), 0)
    col = lax.broadcasted_iota(jnp.int32, (count, total), 1)
    wanted = (row // slots) * (GROUPS * slots) + group * slots + row % slots
    return (col == wanted).astype(jnp.bfloat16)


def unpack_kernel(slots, sources, arrived_ref, rows_ref):
    pick = unpack_rows(slots, sources, pl.program_id(0))
    rows_ref[...] = jnp.dot(
        pick, arrived_ref[...], preferred_element_type=jnp.float32
    ).astype(jnp.bfloat16)


def unpack(arrived, slots, sources):
    packed, width = arrived.shape
    count = slots * sources
    return pl.pallas_call(
        functools.partial(unpack_kernel, slots, sources),
        grid=(GROUPS,),
        in_specs=[pl.BlockSpec((packed, width), lambda g: (0, 0))],
        out_specs=pl.BlockSpec((count, width), lambda g: (0, g)),
        out_shape=jax.ShapeDtypeStruct((count, GROUPS * width), jnp.bfloat16),
        compiler_params=pltpu.CompilerParams(vmem_limit_bytes=58 * 1024 * 1024),
        cost_estimate=pl.CostEstimate(
            flops=2 * GROUPS * count * packed * width,
            bytes_accessed=4 * packed * width,
            transcendentals=0,
        ),
    )(arrived)


def expert_kernel(slots, sources, rows_ref, weight_ref, out_ref, total_ref):
    step = pl.program_id(0)
    width = out_ref.shape[1]
    dims = (((1,), (1,)), ((), ()))
    rows = rows_ref[...]
    gate = lax.dot_general(rows, weight_ref[0], dims, preferred_element_type=jnp.float32)
    upper = lax.dot_general(rows, weight_ref[1], dims, preferred_element_type=jnp.float32)
    hidden = (jax.nn.silu(gate) * upper).astype(jnp.bfloat16)
    part = jnp.dot(hidden, weight_ref[2], preferred_element_type=jnp.float32)

    @pl.when(step == 0)
    def _():
        total_ref[...] = part

    @pl.when(step > 0)
    def _():
        total_ref[...] += part

    @pl.when(step == pl.num_programs(0) - 1)
    def _():
        packed = None
        for group in range(GROUPS):
            block = total_ref[:, group * width : (group + 1) * width].astype(jnp.bfloat16)
            pick = unpack_rows(slots, sources, group)
            term = lax.dot_general(
                pick, block, (((0,), (0,)), ((), ())), preferred_element_type=jnp.float32
            )
            packed = term if packed is None else packed + term
        out_ref[...] = packed.astype(jnp.bfloat16)


def expert_apply(rows, weights, slots, sources, chunk=256):
    count, channels = rows.shape
    units = weights.shape[1]
    packed, width = count * GROUPS, channels // GROUPS
    return pl.pallas_call(
        functools.partial(expert_kernel, slots, sources),
        grid=(units // chunk,),
        in_specs=[
            pl.BlockSpec((count, channels), lambda i: (0, 0)),
            pl.BlockSpec((3, chunk, channels), lambda i: (0, i, 0)),
        ],
        out_specs=pl.BlockSpec((packed, width), lambda i: (0, 0)),
        out_shape=jax.ShapeDtypeStruct((packed, width), jnp.bfloat16),
        scratch_shapes=[pltpu.VMEM((count, channels), jnp.float32)],
        compiler_params=pltpu.CompilerParams(vmem_limit_bytes=58 * 1024 * 1024),
        cost_estimate=pl.CostEstimate(
            flops=6 * count * units * channels,
            bytes_accessed=6 * units * channels + 4 * packed * width,
            transcendentals=count * units,
        ),
    )(rows, weights)


def combine_kernel(slots, spot_ref, gain_ref, returned_ref, out_ref):
    steps_n, packed = out_ref.shape[0], returned_ref.shape[0]
    spots = lax.broadcasted_iota(jnp.int32, (steps_n, packed), 1)
    pick = (spots == spot_ref[...] + pl.program_id(0) * slots).astype(jnp.bfloat16)
    rows = jnp.dot(pick, returned_ref[...], preferred_element_type=jnp.float32)
    out_ref[...] = (gain_ref[...] * rows).astype(jnp.bfloat16)


def combine(spot, gain, returned, slots):
    packed, width = returned.shape
    steps_n = spot.shape[0]
    column = pl.BlockSpec((steps_n, 1), lambda g: (0, 0))
    return pl.pallas_call(
        functools.partial(combine_kernel, slots),
        grid=(GROUPS,),
        in_specs=[column, column, pl.BlockSpec((packed, width), lambda g: (0, 0))],
        out_specs=pl.BlockSpec((steps_n, width), lambda g: (0, g)),
        out_shape=jax.ShapeDtypeStruct((steps_n, GROUPS * width), jnp.bfloat16),
        compiler_params=pltpu.CompilerParams(vmem_limit_bytes=24 * 1024 * 1024),
        cost_estimate=pl.CostEstimate(
            flops=2 * GROUPS * steps_n * packed * width,
            bytes_accessed=2 * packed * width + 2 * GROUPS * steps_n * width,
            transcendentals=0,
        ),
    )(spot, gain, returned)


def presum_kernel(members_ref, column_ref, out_ref, total_ref):
    total_ref[...] = jnp.zeros_like(total_ref)
    for k in range(column_ref.shape[0]):
        total_ref[members_ref[k]] += column_ref[k, 0].astype(jnp.float32)
    out_ref[0] = total_ref[...].astype(jnp.bfloat16)


def presum(members, column, prompts):
    size_x, size_y, rows, lanes = column.shape
    smem = pl.BlockSpec(memory_space=pltpu.SMEM)
    return pl.pallas_call(
        presum_kernel,
        grid=(size_y,),
        in_specs=[smem, pl.BlockSpec((size_x, 1, rows, lanes), lambda i: (0, i, 0, 0))],
        out_specs=pl.BlockSpec((1, prompts, rows, lanes), lambda i: (i, 0, 0, 0)),
        out_shape=jax.ShapeDtypeStruct((size_y, prompts, rows, lanes), jnp.bfloat16),
        scratch_shapes=[pltpu.VMEM((prompts, rows, lanes), jnp.float32)],
        compiler_params=pltpu.CompilerParams(vmem_limit_bytes=16 * 1024 * 1024),
        cost_estimate=pl.CostEstimate(
            flops=size_x * size_y * rows * lanes,
            bytes_accessed=3 * size_x * size_y * rows * lanes,
            transcendentals=0,
        ),
    )(members, column)


def collect_kernel(*refs):
    pieces, (state_ref, taps_ref) = refs[:-2], refs[-2:]
    lanes = state_ref.shape[1]
    total = pieces[0][...].astype(jnp.float32)
    for piece in pieces[1:]:
        total = total + piece[...].astype(jnp.float32)
    state_ref[...] = total[:, :lanes]
    taps_ref[...] = total[:, lanes:]


def collect(pieces):
    prompts, rows, lanes = pieces[0].shape
    vmem = pl.BlockSpec(memory_space=pltpu.VMEM)
    return pl.pallas_call(
        collect_kernel,
        in_specs=[vmem] * len(pieces),
        out_specs=[vmem, vmem],
        out_shape=[
            jax.ShapeDtypeStruct((prompts, rows - 16, lanes), jnp.float32),
            jax.ShapeDtypeStruct((prompts, 16, lanes), jnp.float32),
        ],
        compiler_params=pltpu.CompilerParams(vmem_limit_bytes=16 * 1024 * 1024),
        cost_estimate=pl.CostEstimate(
            flops=len(pieces) * prompts * rows * lanes,
            bytes_accessed=2 * len(pieces) * prompts * rows * lanes,
            transcendentals=0,
        ),
    )(*pieces)


def neighbours(size_x, size_z):
    return [
        [x * size_z + z for x in (low, size_x - 1 - low) for z in range(size_z)]
        for low in range(size_x // 2)
    ]


def shards(
    ssm_input,
    b_inputs,
    c_readout,
    step_raw,
    decay_rate,
    skip_gain,
    conv_weight,
    prompt_state,
    prompt_taps,
    group_index,
    lengths,
    mixed_grad,
    expert_index,
    route_gain,
    gate_weight,
    up_weight,
    down_weight,
):
    steps_n, row_width = ssm_input.shape
    prompts, own_heads, head_size, state_n = prompt_state.shape
    taps_n, lanes = prompt_taps.shape[2] // head_size, own_heads * head_size
    lines, expert_count = lax.axis_size(("xh", "z")), lax.axis_size(("z", "c"))
    state_rows = own_heads * head_size

    stacked = jnp.concatenate([gate_weight, up_weight, down_weight], 0)
    size_x, size_z = lax.axis_size(("xh", "xl")), lax.axis_size("z")
    swap = []
    for x in range(size_x):
        half, other = x // (size_x // 2), size_x - 1 - x
        swap += [(x * 2 + half, x * 2 + half), (x * 2 + 1 - half, other * 2 + half)]
    swapped = lax.ppermute(stacked, ("xh", "xl", "c"), swap)
    weights = lax.all_gather(swapped, ("y", "xl", "c"), axis=1, tiled=True)

    size_y = lax.axis_size("y")
    x_axes = ("xh", "xl")
    x_index = lax.axis_index(x_axes).astype(jnp.int32)
    row = lax.axis_index("y").astype(jnp.int32)[None]

    own_taps = jnp.transpose(
        prompt_taps.reshape(prompts, own_heads, taps_n, head_size), (0, 2, 1, 3)
    ).reshape(prompts, taps_n, lanes)
    held = jnp.concatenate(
        [
            prompt_state.reshape(prompts, state_rows, state_n),
            own_taps,
            jnp.zeros((prompts, 16 - taps_n, lanes), jnp.bfloat16),
        ],
        1,
    )
    column_state = lax.all_to_all(
        jnp.broadcast_to(held[None], (size_y,) + held.shape), "y", 0, 0, tiled=True
    )
    back = [group_index] + [
        lax.ppermute(group_index, x_axes, [(i, (i + d) % size_x) for i in range(size_x)])
        for d in range(1, size_x)
    ]
    behind = jnp.concatenate(back)
    steps_back = (x_index - lax.iota(jnp.int32, size_x)) % size_x
    picked = steps_back[:, None] == lax.iota(jnp.int32, size_x)[None, :]
    row_members = jnp.sum(jnp.where(picked, behind[None, :], 0), axis=1)
    state = lax.all_to_all(
        jnp.where(
            (row_members == 1)[:, None, None, None], column_state[:, 1][None], column_state[:, 0][None]
        ),
        x_axes,
        0,
        0,
        tiled=True,
    )
    prior = jnp.transpose(state[:, :, state_rows : state_rows + taps_n], (2, 1, 0, 3))
    prior = prior.reshape(taps_n, row_width).astype(jnp.float32)
    prior = jnp.concatenate([jnp.zeros((8 - taps_n, row_width), jnp.float32), prior], 0)

    step_size = jax.nn.softplus(step_raw)
    base, outgoing_grad, grow = mixer_base(
        lengths,
        row,
        ssm_input,
        prior,
        conv_weight,
        jnp.repeat(skip_gain, head_size)[None, :],
        mixed_grad,
        b_inputs,
        c_readout,
        step_size,
        decay_rate[None, :],
        head_size,
        (size_y, size_x),
    )

    slots = 3 * steps_n // (2 * expert_count)
    width = row_width // GROUPS
    chosen = expert_index[:, 0]
    order = lax.iota(jnp.int32, steps_n)
    before = (chosen[:, None] == chosen[None, :]) & (order[:, None] < order[None, :])
    slot = jnp.sum(before.astype(jnp.int32), axis=0)
    place = (chosen % 2) * (lines // 2) + chosen // 2
    spot = (place * (GROUPS * slots) + slot)[None, :]
    packed_rows = lines * GROUPS * slots
    outgoing = dispatch(lengths, base, state, c_readout, grow, spot, head_size, slots, packed_rows)
    arrived = lax.all_to_all(
        outgoing.reshape(lines, GROUPS * slots, width),
        LINE,
        0,
        0,
        tiled=True,
        axis_index_groups=neighbours(size_x, size_z),
    )
    arrived, outgoing_grad = lax.optimization_barrier((arrived, outgoing_grad))
    column_grad = lax.all_to_all(outgoing_grad, x_axes, 0, 0, tiled=True)
    expert_rows = unpack(arrived.reshape(packed_rows, width), slots, lines)
    produced = expert_apply(expert_rows, weights, slots, lines)
    produced, column_grad = lax.optimization_barrier((produced, column_grad))
    row_grad = presum(row_members, column_grad, prompts)
    returned = lax.all_to_all(
        produced.reshape(lines, GROUPS * slots, width),
        LINE,
        0,
        0,
        tiled=True,
        axis_index_groups=neighbours(size_x, size_z),
    ).reshape(packed_rows, width)
    pieces = [row_grad[0]] + [
        lax.ppermute(row_grad[d], "y", [(i, (i + d) % size_y) for i in range(size_y)])
        for d in range(1, size_y)
    ]
    state_sum, taps_sum = collect(pieces)
    state_grad = state_sum.reshape(prompts, own_heads, head_size, state_n)
    taps_grad = jnp.transpose(
        taps_sum[:, :taps_n].reshape(prompts, taps_n, own_heads, head_size), (0, 2, 1, 3)
    ).reshape(prompts, own_heads, taps_n * head_size)
    moe_out = combine(jnp.transpose(spot), route_gain, returned, slots)
    return (moe_out, state_grad, taps_grad)


def solution(mesh):
    prompt, dp, expert = (mesh.shape[name] for name in ("prompt", "dp", "expert"))
    fine = Mesh(mesh.devices.reshape(prompt, 2, dp // 2, expert // 2, 2), AXES)
    tokens = P(AXES, None)
    single = P(AXES)
    experts, plane = ("z", "c"), PLANE
    return jax.shard_map(
        shards,
        mesh=fine,
        in_specs=(
            tokens,
            tokens,
            tokens,
            tokens,
            P(),
            P(),
            P(),
            P(experts, plane, None, None),
            P(experts, plane, None),
            single,
            single,
            tokens,
            tokens,
            tokens,
            P(experts, plane, None),
            P(experts, plane, None),
            P(experts, plane, None),
        ),
        out_specs=(
            tokens,
            P(experts, plane, None, None),
            P(experts, plane, None),
        ),
        check_vma=False,
    )
```
